512 devices in a mesh: bl: 64 (over y, z), ta: 8 (over x, core).
Axes of the slice: x: 4, y: 8, z: 8, core: 2. Of those that a mesh axis runs over, the one named last changes fastest.
Arguments:
- visibilities: bfloat16 [128, 16384, 512], P('ta', 'bl'), may hold values from -12 to 12
- flags: int32 [128, 16384], P('ta', 'bl'), may hold values 0 or 1
- group_ids: int32 [16384], P('bl'), may hold values from 0 to 511, as said below
- group_order: int32 [512], replicated, may hold values from 0 to 511, each once
- taper: float32 [256], replicated, may hold values from 0.25 to 1.75
- inv_cov: float32 [256, 256], replicated, may hold values from -1 to 2
Outputs:
- spectrum: float32 [512, 256], P('bl')
The draws below stay inside these ranges and needn't reach their ends.
Inputs may be any that keep to these rules, and one draw needn't show every extreme that they name: `group_ids`: within each block of 256 baselines the ids do not fall; a baseline of block i belongs to a group whose home block id // 8 equals (i - k) mod (64) for some k < 4.
All inputs are finite; a program needn't handle non-finite values. No bound on the sum of `flags` on one device may be relied on, other than what follows from the above.
Results may differ from the reference program's by a relative error of at most 0.00068.
Values may be sent and summed in bfloat16 or wider, within the bound.
No kernel may reach another device: no remote copies, remote signals or barrier semaphores. Data moves between devices by JAX's collectives and lax.ppermute only.
A program may use at most 64 MiB of HBM per device.

```python
import math
import jax
import jax.numpy as jnp
from jax import lax

NCH = 256
BL_DEV = 256
GR_DEV = 8
ROUNDS = 3
SPAN = 4
LG = 32
NG = 512
BLS = 16384
TIMES = 128
N_BL = 64


def shared_groups(key):
    shared_key = jax.random.fold_in(key, 7)
    first_key, second_key, third_key = jax.random.split(shared_key, 3)
    block_total = BLS // BL_DEV
    steps_back = jax.random.randint(first_key, (block_total, BL_DEV), 0, SPAN)
    member = jax.random.randint(second_key, (block_total, BL_DEV), 0, GR_DEV)
    single_member = jax.random.randint(third_key, (block_total,), 0, GR_DEV)
    block_index = jnp.arange(block_total, dtype=jnp.int32)[:, None]
    home_block = (block_index - steps_back) % block_total
    home_single = jnp.take(single_member, home_block)
    redirect = (member == home_single) & (steps_back > 0)
    steps_back = jnp.where(redirect, 0, steps_back)
    home_block = (block_index - steps_back) % block_total
    group_ids = jnp.sort(home_block * GR_DEV + member, axis=1)
    return group_ids.reshape(BLS).astype(jnp.int32)


def draw_group_ids(key, part):
    return shared_groups(key)


def draw_visibilities(key, part):
    group_ids = shared_groups(key)
    key = jax.random.fold_in(key, 2)
    sky_key, noise_key = jax.random.split(key, 2)
    sky_signal = jax.random.normal(sky_key, (TIMES, NG, 2 * NCH), jnp.float32)
    noise_part = 0.7 * jax.random.normal(noise_key, (TIMES, BLS, 2 * NCH), jnp.float32)
    visible = jnp.take(sky_signal, group_ids, axis=1) + noise_part
    return jnp.clip(visible, -12.0, 12.0).astype(jnp.bfloat16)


def draw_inv_cov(key, part):
    key = jax.random.fold_in(key, 3)
    off_key, diag_key = jax.random.split(key)
    raw_part = 0.5 * jax.random.normal(off_key, (NCH, NCH), jnp.float32) / math.sqrt(NCH)
    symmetric = (raw_part + raw_part.T) * 0.7071
    diagonal = jnp.exp(jax.random.uniform(diag_key, (NCH,), jnp.float32, 0.0, math.log(2.0)))
    identity = jnp.eye(NCH, dtype=jnp.float32)
    matrix = symmetric * (1.0 - identity) + diagonal[:, None] * identity
    return jnp.clip(matrix, -1.0, 2.0)


def plant(entries, stream_key, least, top_value):
    spot = [jax.random.randint(jax.random.fold_in(stream_key, axis), (), 0, length) for axis, length in enumerate(entries.shape)]
    widest = entries.shape.index(max(entries.shape))
    beside = spot[:widest] + [(spot[widest] + 1) % entries.shape[widest]] + spot[widest + 1:]
    return entries.at[tuple(spot)].set(least).at[tuple(beside)].set(top_value)


def setup_inputs(seed: int = 0) -> dict:
    seeds = jax.random.split(jax.random.key(seed), 7)
    return {
        "visibilities": draw_visibilities(jax.random.fold_in(seeds[6], 71), 0),
        "flags": plant((jax.random.randint(seeds[1], (TIMES, BLS), 0, 8) < 7).astype(jnp.int32), jax.random.fold_in(seeds[1], 1), 0, 1),
        "group_ids": draw_group_ids(jax.random.fold_in(seeds[6], 71), 0),
        "group_order": jax.random.permutation(seeds[3], NG).astype(jnp.int32),
        "taper": jnp.clip(1.0 + 0.15 * jax.random.normal(seeds[4], (NCH,), jnp.float32), 0.25, 1.75),
        "inv_cov": draw_inv_cov(jax.random.fold_in(seeds[6], 71), 0),
    }


def transform_matrix(taper, inv_cov):
    channels = taper.shape[0]
    ramp = jnp.arange(channels, dtype=jnp.int32)
    phase_index = ramp[:, None] * ramp[None, :] % channels
    angles = 2.0 * math.pi / channels * phase_index.astype(jnp.float32)
    norm_factor = 1.0 / math.sqrt(channels)
    cosines = jnp.cos(angles) * norm_factor
    sines = jnp.sin(angles) * norm_factor
    weighted = taper[:, None] * inv_cov
    cos_part = jnp.dot(weighted, cosines, precision=lax.Precision.HIGHEST, preferred_element_type=jnp.float32)
    sin_part = jnp.dot(weighted, sines, precision=lax.Precision.HIGHEST, preferred_element_type=jnp.float32)
    upper_half = jnp.concatenate([cos_part, -sin_part], axis=1)
    lower_half = jnp.concatenate([sin_part, cos_part], axis=1)
    return jnp.concatenate([upper_half, lower_half], axis=0).astype(jnp.bfloat16)

def reference(visibilities, flags, group_ids, group_order, taper, inv_cov):
    matrix = transform_matrix(taper, inv_cov)
    slot_range = jnp.arange(LG, dtype=jnp.int32)

    def per_block(block):
        start = (block * BL_DEV).astype(jnp.int32)
        block_vis = lax.dynamic_slice_in_dim(visibilities, start, BL_DEV, 1)
        block_ids = lax.dynamic_slice_in_dim(group_ids, start, BL_DEV, 0)
        block_flags = lax.dynamic_slice_in_dim(flags, start, BL_DEV, 1)
        delays = jnp.dot(block_vis.reshape(TIMES * BL_DEV, 2 * NCH), matrix, preferred_element_type=jnp.float32)
        delays = delays.astype(jnp.bfloat16).reshape(TIMES, BL_DEV, 2 * NCH)
        slot_index = (block - block_ids // GR_DEV) % N_BL * GR_DEV + block_ids % GR_DEV
        onehot = slot_index[None, :] == slot_range[:, None]
        group_table = jnp.where(onehot[None], block_flags[:, None, :], 0).astype(jnp.bfloat16)
        sums = jnp.einsum('tsb,tbc->tsc', group_table.astype(jnp.float32), delays.astype(jnp.float32))
        counts = lax.optimization_barrier(jnp.sum(group_table.astype(jnp.float32), axis=-1))
        return (sums.astype(jnp.bfloat16), counts)
    all_sums, all_counts = lax.map(per_block, jnp.arange(N_BL, dtype=jnp.int32))
    cross_power = jnp.zeros((N_BL, LG, NCH), jnp.float32)
    pair_count = jnp.zeros((N_BL, LG), jnp.float32)
    for round_number in range(1, ROUNDS + 1):
        offset = round_number * GR_DEV
        partner_sums = jnp.roll(all_sums, round_number, axis=0)
        partner_counts = jnp.roll(all_counts, round_number, axis=0)
        product = lax.optimization_barrier(jnp.sum(all_sums[:, :, offset:, :].astype(jnp.float32) * partner_sums[:, :, :LG - offset, :].astype(jnp.float32), axis=1))
        power_term = product[:, :, :NCH] + product[:, :, NCH:]
        cross_power = cross_power.at[:, offset:, :].add(power_term)
        count_term = lax.optimization_barrier(jnp.sum(all_counts[:, :, offset:] * partner_counts[:, :, :LG - offset], axis=1))
        pair_count = pair_count.at[:, offset:].add(count_term)
    block_index = jnp.arange(N_BL, dtype=jnp.int32)[:, None]
    groups = (block_index - slot_range[None, :] // GR_DEV) % N_BL * GR_DEV + slot_range[None, :] % GR_DEV
    total = jax.ops.segment_sum(cross_power.reshape(N_BL * LG, NCH), groups.reshape(-1), num_segments=NG)
    count = jax.ops.segment_sum(pair_count.reshape(-1), groups.reshape(-1), num_segments=NG)
    return total[group_order] / jnp.maximum(count[group_order], 1.0)[:, None]
```

```python
import math

import numpy as np
import jax
import jax.numpy as jnp
from jax import lax
from jax.sharding import PartitionSpec as P

GR_DEV = 8
SPAN = 4


def shifted(shard, axis, by):
    devices = lax.axis_size(axis)
    return lax.ppermute(shard, axis, [(i, (i + by) % devices) for i in range(devices)])


def fourier_tables(channels):
    ramp = np.arange(channels)
    angles = 2.0 * math.pi / channels * (ramp[:, None] * ramp[None, :] % channels)
    norm_factor = 1.0 / math.sqrt(channels)
    return (np.cos(angles) * norm_factor).astype(np.float32), (np.sin(angles) * norm_factor).astype(np.float32)


def transform_matrix(taper, inv_cov):
    cosines, sines = fourier_tables(taper.shape[0])
    weighted = taper[:, None] * inv_cov
    both = jnp.dot(
        weighted,
        jnp.asarray(np.concatenate([cosines, sines], axis=1)),
        precision=lax.Precision.HIGHEST,
        preferred_element_type=jnp.float32,
    )
    channels = taper.shape[0]
    cos_part, sin_part = both[:, :channels], both[:, channels:]
    upper_half = jnp.concatenate([cos_part, -sin_part], axis=1)
    lower_half = jnp.concatenate([sin_part, cos_part], axis=1)
    return jnp.concatenate([upper_half, lower_half], axis=0).astype(jnp.bfloat16)


def on_device(visibilities, flags, group_ids, group_order, taper, inv_cov):
    channels = taper.shape[0]
    device_index = lax.axis_index("bl")
    block_total = lax.axis_size("bl")
    time_count, block_length, row_width = visibilities.shape
    slot_count = SPAN * GR_DEV

    slot_index = (device_index - group_ids // GR_DEV) % block_total * GR_DEV + group_ids % GR_DEV
    onehot = slot_index[None, :] == jnp.arange(slot_count, dtype=jnp.int32)[:, None]
    group_table = jnp.where(onehot[None], flags[:, None, :], 0).astype(jnp.bfloat16)
    grouped = jnp.einsum(
        "tsb,tbc->tsc", group_table, visibilities, preferred_element_type=jnp.float32
    ).astype(jnp.bfloat16)
    counts = jnp.sum(group_table.astype(jnp.float32), axis=-1)
    count_rows = jnp.pad(counts.T.astype(jnp.bfloat16), ((0, 0), (0, row_width - time_count)))
    wire = jnp.concatenate([grouped, count_rows[None]], axis=0)

    slabs = [wire[:, k * GR_DEV : (k + 1) * GR_DEV] for k in range(SPAN)]
    far_behind = shifted(slabs[3], "bl", -2)
    behind = shifted(slabs[2], "bl", -1)
    ahead = shifted(slabs[0], "bl", 1)
    parts = [ahead, slabs[1], behind, far_behind]

    matrix = transform_matrix(taper, inv_cov)
    delays = [
        jnp.dot(
            part[:time_count].reshape(time_count * GR_DEV, row_width),
            matrix,
            preferred_element_type=jnp.float32,
        )
        for part in parts
    ]
    part_counts = [part[time_count, :, :time_count].astype(jnp.float32) for part in parts]

    def pair_sum(values):
        before = values[0]
        pairs = values[1] * before
        for value, earlier in ((values[2], values[1]), (values[3], values[2])):
            before = before + earlier
            pairs = pairs + value * before
        return pairs

    power = jnp.sum(pair_sum(delays).reshape(time_count, GR_DEV, row_width), axis=0)
    power = power[:, :channels] + power[:, channels:]
    pair_count = jnp.sum(pair_sum(part_counts), axis=1)
    power, pair_count = lax.psum((power, pair_count), "ta")
    spectrum = power / jnp.maximum(pair_count, 1.0)[:, None]

    table = lax.all_gather(spectrum, "bl", axis=0, tiled=True)
    wanted = lax.dynamic_slice_in_dim(group_order, device_index * GR_DEV, GR_DEV, 0)
    rows = (wanted // GR_DEV + 1) % block_total * GR_DEV + wanted % GR_DEV
    pick = (rows[:, None] == jnp.arange(table.shape[0], dtype=jnp.int32)[None, :]).astype(jnp.float32)
    return jnp.dot(pick, table, precision=lax.Precision.HIGHEST, preferred_element_type=jnp.float32)


def solution(mesh):
    return jax.shard_map(
        on_device,
        mesh=mesh,
        in_specs=(P("ta", "bl", None), P("ta", "bl"), P("bl"), P(), P(), P()),
        out_specs=P("bl", None),
        check_vma=False,
    )
```

```python
import functools
import math

import numpy as np
import jax
import jax.numpy as jnp
from jax import lax
from jax.experimental import pallas as pl
from jax.experimental.pallas import tpu as pltpu
from jax.sharding import Mesh
from jax.sharding import PartitionSpec as P

GR_DEV = 8
HALF = GR_DEV // 2
SPAN = 4
LANES = 128
BLOCK_AXES = ("y", "z")
COUNT_ROWS = 16
STEP_TIMES = 4


def shifted(shard, by):
    devices = lax.axis_size(BLOCK_AXES)
    return lax.ppermute(shard, BLOCK_AXES, [(i, (i + by) % devices) for i in range(devices)])


def exchange(chunks, axis):
    return lax.all_to_all(chunks, axis, 0, 0, tiled=True)


def fourier_table(channels):
    ramp = np.arange(channels)
    angles = 2.0 * math.pi / channels * (ramp[:, None] * ramp[None, :] % channels)
    both = np.concatenate([np.cos(angles), np.sin(angles)], axis=1) / math.sqrt(channels)
    return both.astype(np.float32)


def transform_parts(taper, inv_cov):
    weighted = taper[:, None] * inv_cov
    both = jnp.dot(
        weighted,
        jnp.asarray(fourier_table(taper.shape[0])),
        precision=lax.Precision.HIGHEST,
        preferred_element_type=jnp.float32,
    )
    return both.astype(jnp.bfloat16)


def rolled(rows):
    return jnp.concatenate([rows[HALF:], rows[:HALF]], axis=0)


def group_kernel(block_total, where_ref, ids_ref, flags_ref, vis_ref, a_ref, b_ref, c_ref, d1_ref, d2_ref, cnt_ref):
    step = pl.program_id(0)
    row_width = vis_ref.shape[2]
    ids = ids_ref[...]
    back = where_ref[0] - (ids >> 3)
    back = jnp.where(back < 0, back + block_total, back)
    member = ids & (GR_DEV - 1)
    block = (back - (member >= HALF).astype(jnp.int32)) & (SPAN - 1)
    row = lax.broadcasted_iota(jnp.int32, (SPAN * GR_DEV, ids.shape[1]), 0)
    even = (row == block * GR_DEV + member).astype(jnp.float32)
    odd = (row == block * GR_DEV + (member ^ HALF)).astype(jnp.float32)
    lane = lax.broadcasted_iota(jnp.int32, (SPAN * GR_DEV, LANES), 1)

    @pl.when(step == 0)
    def _():
        cnt_ref[...] = jnp.zeros_like(cnt_ref)

    sums = []
    counts = cnt_ref[...]
    for i in range(STEP_TIMES):
        flag = flags_ref[pl.ds(step * STEP_TIMES + i, 1), :].astype(jnp.float32)
        table = (odd if i % 2 else even) * flag
        sums.append(jnp.dot(table.astype(jnp.bfloat16), vis_ref[i], preferred_element_type=jnp.float32))
        total = jnp.sum(table, axis=1, keepdims=True)
        counts = jnp.where(lane == step * STEP_TIMES + i, total, counts)
    cnt_ref[...] = counts
    rows = pl.ds(pl.multiple_of(step * (STEP_TIMES * GR_DEV), STEP_TIMES * GR_DEV), STEP_TIMES * GR_DEV)
    for block_index, ref in enumerate((a_ref, b_ref, c_ref)):
        span = slice(block_index * GR_DEV, (block_index + 1) * GR_DEV)
        ref[rows, :] = jnp.concatenate([s[span] for s in sums], axis=0).astype(jnp.bfloat16)
    low = lax.broadcasted_iota(jnp.int32, (GR_DEV, row_width), 0) < HALF
    last = [s[3 * GR_DEV :] for s in sums]
    pairs = [(last[i], last[i + 1]) for i in range(0, STEP_TIMES, 2)]
    half_rows = pl.ds(pl.multiple_of(step * (STEP_TIMES * HALF), STEP_TIMES * HALF), STEP_TIMES * HALF)
    d1_ref[half_rows, :] = jnp.concatenate([jnp.where(low, x, y) for x, y in pairs], axis=0).astype(jnp.bfloat16)
    d2_ref[half_rows, :] = jnp.concatenate([jnp.where(low, y, x) for x, y in pairs], axis=0).astype(jnp.bfloat16)

    @pl.when(step == pl.num_programs(0) - 1)
    def _():
        for block_index, ref in enumerate((a_ref, b_ref, c_ref, d1_ref, d2_ref)):
            first = min(block_index, SPAN - 1) * GR_DEV
            mine = counts[first : first + GR_DEV]
            tile = jnp.concatenate([mine, jnp.zeros_like(mine)], axis=0)
            tile = jnp.concatenate([tile, jnp.zeros((COUNT_ROWS, row_width - LANES), jnp.float32)], axis=1)
            ref[ref.shape[0] - COUNT_ROWS :, :] = tile.astype(jnp.bfloat16)


def group_sums(visibilities, flags, group_ids, device_index, block_total):
    time_count, block_length, row_width = visibilities.shape
    full = time_count * GR_DEV + COUNT_ROWS
    part = time_count * HALF + COUNT_ROWS
    shapes = [full, full, full, part, part]
    return pl.pallas_call(
        functools.partial(group_kernel, block_total),
        grid_spec=pltpu.PrefetchScalarGridSpec(
            num_scalar_prefetch=1,
            grid=(time_count // STEP_TIMES,),
            in_specs=[
                pl.BlockSpec((1, block_length), lambda i, s: (0, 0)),
                pl.BlockSpec((time_count, block_length), lambda i, s: (0, 0)),
                pl.BlockSpec((STEP_TIMES, block_length, row_width), lambda i, s: (i, 0, 0)),
            ],
            out_specs=[pl.BlockSpec((n, row_width), lambda i, s: (0, 0)) for n in shapes],
            scratch_shapes=[pltpu.VMEM((SPAN * GR_DEV, LANES), jnp.float32)],
        ),
        out_shape=[jax.ShapeDtypeStruct((n, row_width), jnp.bfloat16) for n in shapes],
        compiler_params=pltpu.CompilerParams(vmem_limit_bytes=57 << 20),
        cost_estimate=pl.CostEstimate(
            flops=2 * time_count * SPAN * GR_DEV * block_length * row_width,
            bytes_accessed=visibilities.size * 2,
            transcendentals=0,
        ),
        name="group_sums",
    )(device_index[None], group_ids[None, :], flags, visibilities)


def pair_sum(a, b, c, d):
    return b * a + c * (a + b) + d * (a + b + c)


def power_kernel(parts_ref, a_ref, b_ref, c_ref, d1_ref, d2_ref, out_ref):
    channels = parts_ref.shape[0]
    time_count = (a_ref.shape[0] - COUNT_ROWS) // GR_DEV
    cosines = parts_ref[:, :channels]
    sines = parts_ref[:, channels:]

    def dot(x, y):
        return jnp.dot(x, y, preferred_element_type=jnp.float32)

    def delays(ref):
        rows = ref.shape[0] - COUNT_ROWS
        re, im = ref[:rows, :channels], ref[:rows, channels:]
        return dot(re, cosines) + dot(im, sines), dot(im, cosines) - dot(re, sines)

    low = lax.broadcasted_iota(jnp.int32, (GR_DEV, channels), 0) < HALF
    power = [jnp.zeros((GR_DEV, channels), jnp.float32) for _ in range(2)]
    for a, b, c, d1, d2 in zip(*(delays(ref) for ref in (a_ref, b_ref, c_ref, d1_ref, d2_ref))):
        for t in range(time_count):
            at = slice(t * GR_DEV, (t + 1) * GR_DEV)
            half_at = slice(t // 2 * GR_DEV, (t // 2 + 1) * GR_DEV)
            first, second = (d2, d1) if t % 2 else (d1, d2)
            d = jnp.where(low, first[half_at], second[half_at])
            power[t % 2] = power[t % 2] + pair_sum(a[at], b[at], c[at], d)
    power = power[0] + rolled(power[1])

    counts = []
    for ref in (a_ref, b_ref, c_ref, d1_ref, d2_ref):
        first = ref.shape[0] - COUNT_ROWS
        counts.append(ref[first:, :LANES].astype(jnp.float32)[:GR_DEV])
    row = lax.broadcasted_iota(jnp.int32, (GR_DEV, LANES), 0)
    even = lax.broadcasted_iota(jnp.int32, (GR_DEV, LANES), 1) % 2 == 0
    d = jnp.where((row < HALF) == even, counts[3], counts[4])
    pairs = pair_sum(counts[0], counts[1], counts[2], d)
    pairs = jnp.where(even, pairs, 0.0) + rolled(jnp.where(even, 0.0, pairs))
    count = jnp.broadcast_to(jnp.sum(pairs, axis=1, keepdims=True), (GR_DEV, LANES))
    rows = jnp.concatenate([power, count], axis=1)
    for copy in range(out_ref.shape[0]):
        out_ref[copy] = rows


def power_rows(parts, blocks, copies):
    channels = parts.shape[0]
    rows = sum(block.shape[0] - COUNT_ROWS for block in blocks)
    return pl.pallas_call(
        power_kernel,
        out_shape=jax.ShapeDtypeStruct((copies, GR_DEV, channels + LANES), jnp.float32),
        compiler_params=pltpu.CompilerParams(vmem_limit_bytes=16 << 20),
        cost_estimate=pl.CostEstimate(flops=8 * rows * channels * channels, bytes_accessed=2 << 20, transcendentals=0),
        name="power_rows",
    )(parts, *blocks)


def spectrum_kernel(in_ref, out_ref):
    channels = out_ref.shape[2]
    total = in_ref[0]
    for source in range(1, in_ref.shape[0]):
        total = total + in_ref[source]
    count = jnp.maximum(total[:, channels:], 1.0)
    count = jnp.concatenate([count] * (channels // LANES), axis=1)
    spectrum = total[:, :channels] / count
    for copy in range(out_ref.shape[0]):
        out_ref[copy] = spectrum


def spectrum_rows(partial_rows, channels, copies):
    return pl.pallas_call(
        spectrum_kernel,
        out_shape=jax.ShapeDtypeStruct((copies, GR_DEV, channels), jnp.float32),
        name="spectrum_rows",
    )(partial_rows)


def on_device(visibilities, flags, group_ids, group_order, taper, inv_cov):
    channels = taper.shape[0]
    y_size, z_size = lax.axis_size("y"), lax.axis_size("z")
    block_total = y_size * z_size
    device_index = lax.axis_index(BLOCK_AXES)

    a, b, c, d1, d2 = group_sums(visibilities, flags, group_ids, device_index, block_total)
    d1, d2 = shifted(d1, -2), shifted(d2, 2)
    c, a = shifted(c, -1), shifted(a, 1)
    parts = transform_parts(taper, inv_cov)
    rows = power_rows(parts, (a, b, c, d1, d2), lax.axis_size("ta"))

    spectrum = spectrum_rows(exchange(rows, "ta"), channels, z_size)

    plane = exchange(spectrum, "z").reshape(z_size * GR_DEV, channels)
    order = group_order.reshape(y_size, z_size, GR_DEV)
    wanted = lax.dynamic_index_in_dim(order, lax.axis_index("z"), 1, keepdims=False).reshape(-1)
    member = wanted % GR_DEV
    holder = (wanted // GR_DEV + jnp.where(member < HALF, 1, 2)) % block_total
    place = jnp.where(holder // z_size == lax.axis_index("y"), holder % z_size * GR_DEV + member, -1)
    pick = (place[:, None] == jnp.arange(z_size * GR_DEV, dtype=jnp.int32)[None, :]).astype(jnp.float32)
    chosen = jnp.dot(pick, plane, precision=lax.Precision.HIGHEST, preferred_element_type=jnp.float32)
    return jnp.sum(exchange(chosen.reshape(y_size, GR_DEV, channels), "y"), axis=0)


def solution(mesh):
    blocks, times = mesh.devices.shape
    y_size = 2 ** (int(math.log2(blocks)) // 2)
    cut = Mesh(mesh.devices.reshape(y_size, blocks // y_size, times), ("y", "z", "ta"))
    return jax.shard_map(
        on_device,
        mesh=cut,
        in_specs=(P("ta", BLOCK_AXES, None), P("ta", BLOCK_AXES), P(BLOCK_AXES), P(), P(), P()),
        out_specs=P(BLOCK_AXES, None),
        check_vma=False,
    )
```

```python
import functools
import math

import numpy as np
import jax
import jax.numpy as jnp
from jax import lax
from jax.experimental import pallas as pl
from jax.experimental.pallas import tpu as pltpu
from jax.sharding import Mesh
from jax.sharding import PartitionSpec as P

GR_DEV = 8
SPAN = 4
LANES = 128
BLOCK_AXES = ("y", "z")
COUNT_ROWS = 16
SLICE = 32
PACK = 4


def shifted(shard, by):
    devices = lax.axis_size(BLOCK_AXES)
    return lax.ppermute(shard, BLOCK_AXES, [(i, (i + by) % devices) for i in range(devices)])


def exchange(chunks, axis):
    return lax.all_to_all(chunks, axis, 0, 0, tiled=True)


def fourier_table(channels):
    ramp = np.arange(channels)
    angles = 2.0 * math.pi / channels * (ramp[:, None] * ramp[None, :] % channels)
    both = np.concatenate([np.cos(angles), np.sin(angles)], axis=1) / math.sqrt(channels)
    return both.astype(np.float32)


def exact_dot(x, y):
    return jnp.dot(x, y, precision=lax.Precision.HIGHEST, preferred_element_type=jnp.float32)


def transform_parts(taper, inv_cov):
    weighted = taper[:, None] * inv_cov
    return exact_dot(weighted, jnp.asarray(fourier_table(taper.shape[0]))).astype(jnp.bfloat16)


STEPS_BACK = (3, 2, 0, 1)


def group_kernel(block_total, place_ref, ids_ref, flags_ref, vis_ref, *rest):
    *refs, held_ref, sems = rest
    time_count, _, row_width = vis_ref.shape
    copies = [pltpu.make_async_copy(vis_ref.at[t], held_ref.at[t], sems.at[t]) for t in range(time_count)]
    for copy in copies:
        copy.start()
    ids = ids_ref[...]
    back = place_ref[0] - (ids >> 3)
    back = jnp.where(back < 0, back + block_total, back)
    row = lax.broadcasted_iota(jnp.int32, (SPAN * GR_DEV, ids.shape[1]), 0)
    onehot = (row == back * GR_DEV + (ids & (GR_DEV - 1))).astype(jnp.float32)
    lane = lax.broadcasted_iota(jnp.int32, (SPAN * GR_DEV, LANES), 1)
    counts = jnp.zeros((SPAN * GR_DEV, LANES), jnp.float32)
    pending = []
    for t in range(time_count):
        table = onehot * flags_ref[t : t + 1, :].astype(jnp.float32)
        counts = jnp.where(lane == t, jnp.sum(table, axis=1, keepdims=True), counts)
        copies[t].wait()
        pending.append(jnp.dot(table.astype(jnp.bfloat16), held_ref[t], preferred_element_type=jnp.float32))
        if len(pending) == 2:
            for block, ref in zip(STEPS_BACK, refs):
                span = slice(block * GR_DEV, (block + 1) * GR_DEV)
                both = jnp.concatenate([sums[span] for sums in pending], axis=0)
                ref[(t - 1) * GR_DEV : (t + 1) * GR_DEV, :] = both.astype(jnp.bfloat16)
            pending = []
    for block, ref in zip(STEPS_BACK, refs):
        mine = counts[block * GR_DEV : (block + 1) * GR_DEV]
        tile = jnp.concatenate([mine, jnp.zeros_like(mine)], axis=0)
        tile = jnp.concatenate([tile, jnp.zeros((COUNT_ROWS, row_width - LANES), jnp.float32)], axis=1)
        ref[time_count * GR_DEV :, :] = tile.astype(jnp.bfloat16)


def group_sums(visibilities, flags, group_ids, place, block_total):
    time_count, block_length, row_width = visibilities.shape
    shape = jax.ShapeDtypeStruct((time_count * GR_DEV + COUNT_ROWS, row_width), jnp.bfloat16)
    vmem = pl.BlockSpec(memory_space=pltpu.VMEM)
    return pl.pallas_call(
        functools.partial(group_kernel, block_total),
        in_specs=[pl.BlockSpec(memory_space=pltpu.SMEM), vmem, vmem, pl.BlockSpec(memory_space=pltpu.HBM)],
        out_specs=[vmem] * SPAN,
        out_shape=[shape] * SPAN,
        scratch_shapes=[
            pltpu.VMEM(visibilities.shape, visibilities.dtype),
            pltpu.SemaphoreType.DMA((time_count,)),
        ],
        compiler_params=pltpu.CompilerParams(vmem_limit_bytes=50 << 20),
        cost_estimate=pl.CostEstimate(
            flops=2 * time_count * SPAN * GR_DEV * block_length * row_width,
            bytes_accessed=visibilities.size * 2,
            transcendentals=0,
        ),
        name="group_sums",
    )(place, group_ids[None, :], flags, visibilities)


def pair_sum(a, b, c, d):
    return b * a + c * (a + b) + d * (a + b + c)


def lane_group(shape):
    return lax.broadcasted_iota(jnp.int32, shape, len(shape) - 1) // SLICE


def turned(rows, groups):
    return pltpu.roll(rows, groups % PACK * SLICE, 1) if groups % PACK else rows


def packed(rows, slice_index):
    group = lane_group(rows.shape)
    member = lax.broadcasted_iota(jnp.int32, rows.shape, 0) % PACK
    kept = jnp.zeros_like(rows)
    for b in range(PACK):
        kept = jnp.where((group == b) & (member == b), turned(rows, b - slice_index), kept)
    return jnp.concatenate(
        [jnp.sum(kept[a * PACK : (a + 1) * PACK], axis=0, keepdims=True) for a in range(2)], axis=0
    )


def power_kernel(parts_ref, d_ref, c_ref, a_ref, b_ref, out_ref):
    channels = parts_ref.shape[0]
    rows = a_ref.shape[0] - COUNT_ROWS
    slices = channels // SLICE
    cosines = parts_ref[:, :channels]
    sines = parts_ref[:, channels:]

    def dot(x, y):
        return jnp.dot(x, y, preferred_element_type=jnp.float32)

    def delays(ref):
        re, im = ref[:rows, :channels], ref[:rows, channels:]
        return dot(re, cosines) + dot(im, sines), dot(im, cosines) - dot(re, sines)

    blocks = [delays(ref) for ref in (a_ref, b_ref, c_ref, d_ref)]
    pairs = pair_sum(*(re for re, _ in blocks)) + pair_sum(*(im for _, im in blocks))
    power = jnp.sum(pairs.reshape(rows // GR_DEV, GR_DEV, channels), axis=0)
    counts = [ref[rows:, :LANES].astype(jnp.float32)[:GR_DEV] for ref in (a_ref, b_ref, c_ref, d_ref)]
    count = jnp.sum(pair_sum(*counts), axis=1, keepdims=True)
    count = packed(jnp.broadcast_to(count, (GR_DEV, LANES)), 0)
    for j in range(slices):
        half = power[:, j // PACK * LANES : (j // PACK + 1) * LANES]
        chunk = jnp.concatenate([packed(half, j % PACK), count], axis=0)
        for copy in range(out_ref.shape[0] // slices):
            out_ref[copy * slices + j] = chunk


def choose_kernel(times, spot_ref, in_ref, out_ref):
    spectrum = []
    for z in range(in_ref.shape[0] // times):
        total = in_ref[z * times]
        for time in range(1, times):
            total = total + in_ref[z * times + time]
        spectrum.append(total[:2] / jnp.maximum(total[2:], 1.0))
    spectrum = jnp.concatenate(spectrum, axis=0)
    first = lane_group(spectrum.shape) == 0
    rows = jnp.concatenate([jnp.where(first, turned(spectrum, -b), 0.0) for b in range(PACK)], axis=0)
    column = lax.broadcasted_iota(jnp.int32, (spot_ref.shape[0], rows.shape[0]), 1)
    pick = (spot_ref[...] == column).astype(jnp.float32)
    chosen = exact_dot(pick, rows)
    size = chosen.shape[0] // PACK
    chunks = turned(chosen[:size], 0)
    for b in range(1, PACK):
        chunks = chunks + turned(chosen[b * size : (b + 1) * size], b)
    copies = out_ref.shape[0] // (size // 2)
    for y in range(size // 2):
        for copy in range(copies):
            out_ref[y * copies + copy] = chunks[2 * y : 2 * y + 2]


def unpack_kernel(in_ref, out_ref):
    slices = out_ref.shape[1] // SLICE
    group = lane_group((GR_DEV, LANES))
    member = lax.broadcasted_iota(jnp.int32, (GR_DEV, LANES), 0) % PACK
    for half in range(slices // PACK):
        result = jnp.zeros((GR_DEV, LANES), jnp.float32)
        for k in range(PACK):
            j = half * PACK + k
            total = in_ref[j]
            for y in range(1, in_ref.shape[0] // slices):
                total = total + in_ref[y * slices + j]
            total = jnp.concatenate(
                [jnp.broadcast_to(total[a : a + 1], (PACK, LANES)) for a in range(2)], axis=0
            )
            for b in range(PACK):
                result = jnp.where((group == k) & (member == b), turned(total, k - b), result)
        out_ref[:, half * LANES : (half + 1) * LANES] = result


def small_call(kernel, shape, name):
    return pl.pallas_call(
        kernel,
        out_shape=jax.ShapeDtypeStruct(shape, jnp.float32),
        compiler_params=pltpu.CompilerParams(vmem_limit_bytes=16 << 20),
        name=name,
    )


def on_device(visibilities, flags, group_ids, group_order, taper, inv_cov):
    channels = taper.shape[0]
    y_size, z_size, times = (lax.axis_size(axis) for axis in ("y", "z", "ta"))
    block_total = y_size * z_size
    slices = channels // SLICE

    place = lax.axis_index(BLOCK_AXES)[None]
    d, c, a, b = group_sums(visibilities, flags, group_ids, place, block_total)
    d, c, a = shifted(d, -2), shifted(c, -1), shifted(a, 1)
    parts = transform_parts(taper, inv_cov)
    power = small_call(power_kernel, (z_size * slices, 4, LANES), "power_rows")(parts, d, c, a, b)

    gathered = exchange(power, ("z", "ta"))
    order = group_order.reshape(y_size, z_size, 2, PACK)
    wanted = lax.dynamic_index_in_dim(order, lax.axis_index("z"), 1, keepdims=False)
    wanted = wanted.transpose(2, 0, 1).reshape(-1, 1)
    holder = (wanted // GR_DEV + 1) % block_total
    member = wanted % GR_DEV
    spot = (member % PACK * z_size + holder % z_size) * 2 + member // PACK
    spot = jnp.where(holder // z_size == lax.axis_index("y"), spot, -1)
    choose = functools.partial(choose_kernel, times)
    chosen = small_call(choose, (y_size * times, 2, LANES), "choose_rows")(spot, gathered)

    found = exchange(chosen, ("y", "ta"))
    return small_call(unpack_kernel, (GR_DEV, channels), "unpack_rows")(found)


def solution(mesh):
    blocks, times = mesh.devices.shape
    y_size = 2 ** (int(math.log2(blocks)) // 2)
    cut = Mesh(mesh.devices.reshape(y_size, blocks // y_size, times), ("y", "z", "ta"))
    return jax.shard_map(
        on_device,
        mesh=cut,
        in_specs=(P("ta", BLOCK_AXES, None), P("ta", BLOCK_AXES), P(BLOCK_AXES), P(), P(), P()),
        out_specs=P(BLOCK_AXES, None),
        check_vma=False,
    )
```

```python
import functools
import math

import numpy as np
import jax
import jax.numpy as jnp
from jax import lax
from jax.experimental import pallas as pl
from jax.experimental.pallas import tpu as pltpu
from jax.sharding import Mesh
from jax.sharding import PartitionSpec as P

GR_DEV = 8
SPAN = 4
LANES = 128
BLOCK_AXES = ("y", "z")
COUNT_ROWS = 16
TOGETHER = 4


def opposed(shard, by):
    blocks, times = lax.axis_size(BLOCK_AXES), lax.axis_size("ta")
    pairs = []
    for block in range(blocks):
        for time in range(times):
            target = (block + (-by if time % 2 else by)) % blocks
            pairs.append((block * times + time, target * times + time))
    return lax.ppermute(shard, (*BLOCK_AXES, "ta"), pairs)


def exchange(chunks, axis):
    return lax.all_to_all(chunks, axis, 0, 0, tiled=True)


def fourier_table(channels):
    ramp = np.arange(channels)
    angles = 2.0 * math.pi / channels * (ramp[:, None] * ramp[None, :] % channels)
    both = np.concatenate([np.cos(angles), np.sin(angles)], axis=1) / math.sqrt(channels)
    return both.astype(np.float32)


def exact_dot(x, y):
    return jnp.dot(x, y, precision=lax.Precision.HIGHEST, preferred_element_type=jnp.float32)


def transform_parts(taper, inv_cov):
    weighted = taper[:, None] * inv_cov
    return exact_dot(weighted, jnp.asarray(fourier_table(taper.shape[0]))).astype(jnp.bfloat16)


BLOCK_STEPS = (3, 2, 0, 1)


def group_kernel(block_total, place_ref, ids_hbm, flags_hbm, vis_hbm, *rest):
    *refs, ids_ref, flags_ref, held_ref, few_sems, sems = rest
    time_count, _, row_width = vis_hbm.shape
    few = [
        pltpu.make_async_copy(source, target, few_sems.at[i])
        for i, (source, target) in enumerate(((ids_hbm, ids_ref), (flags_hbm, flags_ref)))
    ]
    copies = [pltpu.make_async_copy(vis_hbm.at[t], held_ref.at[t], sems.at[t]) for t in range(time_count)]
    for copy in few + copies:
        copy.start()
    for copy in few:
        copy.wait()
    ids = ids_ref[...]
    back = place_ref[0] - (ids >> 3)
    back = jnp.where(back < 0, back + block_total, back)
    back = jnp.where(place_ref[1] == 1, SPAN - 1 - back, back)
    row = lax.broadcasted_iota(jnp.int32, (SPAN * GR_DEV, ids.shape[1]), 0)
    onehot = (row == back * GR_DEV + (ids & (GR_DEV - 1))).astype(jnp.float32)
    lane = lax.broadcasted_iota(jnp.int32, (SPAN * GR_DEV, LANES), 1)
    counts = jnp.zeros((SPAN * GR_DEV, LANES), jnp.float32)
    for first in range(0, time_count, TOGETHER):
        tables = []
        for t in range(first, first + TOGETHER):
            table = onehot * flags_ref[t : t + 1, :].astype(jnp.float32)
            counts = jnp.where(lane == t, jnp.sum(table, axis=1, keepdims=True), counts)
            tables.append(table.astype(jnp.bfloat16))
        for t in range(first, first + TOGETHER):
            copies[t].wait()
        sums = [
            jnp.dot(table, held_ref[first + i], preferred_element_type=jnp.float32)
            for i, table in enumerate(tables)
        ]
        for step, ref in zip(BLOCK_STEPS, refs):
            span = slice(step * GR_DEV, (step + 1) * GR_DEV)
            both = jnp.concatenate([one[span] for one in sums], axis=0)
            ref[first * GR_DEV : (first + TOGETHER) * GR_DEV, :] = both.astype(jnp.bfloat16)
    for step, ref in zip(BLOCK_STEPS, refs):
        mine = counts[step * GR_DEV : (step + 1) * GR_DEV]
        tile = jnp.concatenate([mine, jnp.zeros_like(mine)], axis=0)
        tile = jnp.concatenate([tile, jnp.zeros((COUNT_ROWS, row_width - LANES), jnp.float32)], axis=1)
        ref[time_count * GR_DEV :, :] = tile.astype(jnp.bfloat16)


def group_sums(visibilities, flags, group_ids, place, block_total):
    time_count, block_length, row_width = visibilities.shape
    block = pltpu.VMEM((time_count * GR_DEV + COUNT_ROWS, row_width), jnp.bfloat16)
    arrays = [pltpu.with_memory_space_constraint(x, pltpu.HBM) for x in (group_ids[None, :], flags, visibilities)]
    return pl.pallas_call(
        functools.partial(group_kernel, block_total),
        in_specs=[pl.BlockSpec(memory_space=pltpu.SMEM)] + [pl.BlockSpec(memory_space=pltpu.HBM)] * len(arrays),
        out_specs=[pl.BlockSpec(memory_space=pltpu.VMEM)] * SPAN,
        out_shape=[block] * SPAN,
        scratch_shapes=[pltpu.VMEM(x.shape, x.dtype) for x in arrays]
        + [pltpu.SemaphoreType.DMA((2,)), pltpu.SemaphoreType.DMA((time_count,))],
        compiler_params=pltpu.CompilerParams(vmem_limit_bytes=16 << 20),
        cost_estimate=pl.CostEstimate(
            flops=2 * time_count * SPAN * GR_DEV * block_length * row_width,
            bytes_accessed=visibilities.size * 2,
            transcendentals=0,
        ),
        name="group_sums",
    )(place, *arrays)


def pair_sum(a, b, c, d):
    return b * a + c * (a + b) + d * (a + b + c)


def power_kernel(parts_ref, a_ref, b_ref, c_ref, d_ref, out_ref):
    channels = parts_ref.shape[0]
    rows = a_ref.shape[0] - COUNT_ROWS
    cosines = parts_ref[:, :channels]
    sines = parts_ref[:, channels:]

    def dot(x, y):
        return jnp.dot(x, y, preferred_element_type=jnp.float32)

    def delays(ref):
        re, im = ref[:rows, :channels], ref[:rows, channels:]
        return dot(re, cosines) + dot(im, sines), dot(im, cosines) - dot(re, sines)

    blocks = [delays(ref) for ref in (a_ref, b_ref, c_ref, d_ref)]
    pairs = pair_sum(*(re for re, _ in blocks)) + pair_sum(*(im for _, im in blocks))
    power = jnp.sum(pairs.reshape(rows // GR_DEV, GR_DEV, channels), axis=0)
    counts = [ref[rows:, :LANES].astype(jnp.float32)[:GR_DEV] for ref in (a_ref, b_ref, c_ref, d_ref)]
    count = jnp.sum(pair_sum(*counts), axis=1, keepdims=True)
    result = jnp.concatenate([power, jnp.broadcast_to(count, (GR_DEV, LANES))], axis=1)
    for copy in range(out_ref.shape[0]):
        out_ref[copy] = result


def power_rows(parts, blocks, copies):
    channels = parts.shape[0]
    rows = sum(block.shape[0] - COUNT_ROWS for block in blocks)
    return pl.pallas_call(
        power_kernel,
        out_shape=jax.ShapeDtypeStruct((copies, GR_DEV, channels + LANES), jnp.float32),
        compiler_params=pltpu.CompilerParams(vmem_limit_bytes=16 << 20),
        cost_estimate=pl.CostEstimate(flops=8 * rows * channels * channels, bytes_accessed=2 << 20, transcendentals=0),
        name="power_rows",
    )(parts, *blocks)


def on_device(visibilities, flags, group_ids, group_order, taper, inv_cov):
    channels = taper.shape[0]
    y_size, z_size, times = (lax.axis_size(axis) for axis in ("y", "z", "ta"))
    block_total = y_size * z_size
    core = lax.axis_index("ta") % 2
    place = jnp.stack([lax.axis_index(BLOCK_AXES), core])

    blocks = group_sums(visibilities, flags, group_ids, place, block_total)
    blocks = [opposed(block, by) if by else block for block, by in zip(blocks, (-2, -1, 1, 0))]
    rows = power_rows(transform_parts(taper, inv_cov), blocks, z_size)

    plane = exchange(rows, "z").reshape(z_size * GR_DEV, channels + LANES)
    order = group_order.reshape(y_size, z_size, GR_DEV)
    wanted = lax.dynamic_index_in_dim(order, lax.axis_index("z"), 1, keepdims=False).reshape(-1)
    holder = (wanted // GR_DEV + 1 + core) % block_total
    spot = jnp.where(
        holder // z_size == lax.axis_index("y"), holder % z_size * GR_DEV + wanted % GR_DEV, -1
    )
    pick = spot[:, None] == jnp.arange(z_size * GR_DEV, dtype=jnp.int32)[None, :]
    chosen = exact_dot(pick.astype(jnp.float32), plane).reshape(y_size, GR_DEV, channels + LANES)
    found = exchange(chosen, "y").reshape(y_size * GR_DEV, channels + LANES)

    fold = np.tile(np.eye(GR_DEV, dtype=np.float32), (times, y_size))
    partial = exact_dot(jnp.asarray(fold), found).reshape(times, GR_DEV, channels + LANES)
    totals = jnp.sum(exchange(partial, "ta"), axis=0)
    return totals[:, :channels] / jnp.maximum(totals[:, channels : channels + 1], 1.0)


def solution(mesh):
    blocks, times = mesh.devices.shape
    y_size = 2 ** (int(math.log2(blocks)) // 2)
    cut = Mesh(mesh.devices.reshape(y_size, blocks // y_size, times), ("y", "z", "ta"))
    return jax.shard_map(
        on_device,
        mesh=cut,
        in_specs=(P("ta", BLOCK_AXES, None), P("ta", BLOCK_AXES), P(BLOCK_AXES), P(), P(), P()),
        out_specs=P(BLOCK_AXES, None),
        check_vma=False,
    )
```

```python
import functools
import math

import numpy as np
import jax
import jax.numpy as jnp
from jax import lax
from jax.experimental import pallas as pl
from jax.experimental.pallas import tpu as pltpu
from jax.sharding import Mesh
from jax.sharding import PartitionSpec as P

GR_DEV = 8
SPAN = 4
LANES = 128
BLOCK_AXES = ("y", "z")
COUNT_ROWS = 16
SLICE = 32
PACK = 4
TOGETHER = 8


def shifted(shard, by):
    devices = lax.axis_size(BLOCK_AXES)
    return lax.ppermute(shard, BLOCK_AXES, [(i, (i + by) % devices) for i in range(devices)])


def exchange(chunks, axis):
    return lax.all_to_all(chunks, axis, 0, 0, tiled=True)


def fourier_table(channels):
    ramp = np.arange(channels)
    angles = 2.0 * math.pi / channels * (ramp[:, None] * ramp[None, :] % channels)
    both = np.concatenate([np.cos(angles), np.sin(angles)], axis=1) / math.sqrt(channels)
    return both.astype(np.float32)


def exact_dot(x, y):
    return jnp.dot(x, y, precision=lax.Precision.HIGHEST, preferred_element_type=jnp.float32)


def transform_parts(taper, inv_cov):
    weighted = taper[:, None] * inv_cov
    return exact_dot(weighted, jnp.asarray(fourier_table(taper.shape[0]))).astype(jnp.bfloat16)


BLOCK_STEPS = (3, 2, 0, 1)


def group_kernel(block_total, place_ref, ids_hbm, flags_hbm, vis_hbm, *rest):
    *refs, ids_ref, flags_ref, held_ref, few_sems, sems = rest
    time_count, _, row_width = vis_hbm.shape
    few = [
        pltpu.make_async_copy(source, target, few_sems.at[i])
        for i, (source, target) in enumerate(((ids_hbm, ids_ref), (flags_hbm, flags_ref)))
    ]
    copies = [pltpu.make_async_copy(vis_hbm.at[t], held_ref.at[t], sems.at[t]) for t in range(time_count)]
    for copy in few + copies:
        copy.start()
    for copy in few:
        copy.wait()
    ids = ids_ref[...]
    back = place_ref[0] - (ids >> 3)
    back = jnp.where(back < 0, back + block_total, back)
    row = lax.broadcasted_iota(jnp.int32, (SPAN * GR_DEV, ids.shape[1]), 0)
    onehot = (row == back * GR_DEV + (ids & (GR_DEV - 1))).astype(jnp.float32)
    lane = lax.broadcasted_iota(jnp.int32, (SPAN * GR_DEV, LANES), 1)
    counts = jnp.zeros((SPAN * GR_DEV, LANES), jnp.float32)
    for first in range(0, time_count, TOGETHER):
        tables = []
        for t in range(first, first + TOGETHER):
            table = onehot * flags_ref[t : t + 1, :].astype(jnp.float32)
            counts = jnp.where(lane == t, jnp.sum(table, axis=1, keepdims=True), counts)
            tables.append(table.astype(jnp.bfloat16))
        for t in range(first, first + TOGETHER):
            copies[t].wait()
        sums = [
            jnp.dot(table, held_ref[first + i], preferred_element_type=jnp.float32)
            for i, table in enumerate(tables)
        ]
        for step, ref in zip(BLOCK_STEPS, refs):
            span = slice(step * GR_DEV, (step + 1) * GR_DEV)
            both = jnp.concatenate([one[span] for one in sums], axis=0)
            ref[first * GR_DEV : (first + TOGETHER) * GR_DEV, :] = both.astype(jnp.bfloat16)
    for step, ref in zip(BLOCK_STEPS, refs):
        mine = counts[step * GR_DEV : (step + 1) * GR_DEV]
        tile = jnp.concatenate([mine, jnp.zeros_like(mine)], axis=0)
        tile = jnp.concatenate([tile, jnp.zeros((COUNT_ROWS, row_width - LANES), jnp.float32)], axis=1)
        ref[time_count * GR_DEV :, :] = tile.astype(jnp.bfloat16)


def group_sums(visibilities, flags, group_ids, place, block_total):
    time_count, block_length, row_width = visibilities.shape
    block = pltpu.VMEM((time_count * GR_DEV + COUNT_ROWS, row_width), jnp.bfloat16)
    arrays = [pltpu.with_memory_space_constraint(x, pltpu.HBM) for x in (group_ids[None, :], flags, visibilities)]
    return pl.pallas_call(
        functools.partial(group_kernel, block_total),
        in_specs=[pl.BlockSpec(memory_space=pltpu.SMEM)] + [pl.BlockSpec(memory_space=pltpu.HBM)] * len(arrays),
        out_specs=[pl.BlockSpec(memory_space=pltpu.VMEM)] * SPAN,
        out_shape=[block] * SPAN,
        scratch_shapes=[pltpu.VMEM(x.shape, x.dtype) for x in arrays]
        + [pltpu.SemaphoreType.DMA((2,)), pltpu.SemaphoreType.DMA((time_count,))],
        compiler_params=pltpu.CompilerParams(vmem_limit_bytes=16 << 20),
        cost_estimate=pl.CostEstimate(
            flops=2 * time_count * SPAN * GR_DEV * block_length * row_width,
            bytes_accessed=visibilities.size * 2,
            transcendentals=0,
        ),
        name="group_sums",
    )(place, *arrays)


def pair_sum(a, b, c, d):
    return b * a + c * (a + b) + d * (a + b + c)


def lane_group(shape):
    return lax.broadcasted_iota(jnp.int32, shape, len(shape) - 1) // SLICE


def turned(rows, groups):
    return pltpu.roll(rows, groups % PACK * SLICE, 1) if groups % PACK else rows


def packed(rows, slice_index):
    group = lane_group(rows.shape)
    member = lax.broadcasted_iota(jnp.int32, rows.shape, 0) % PACK
    kept = jnp.zeros_like(rows)
    for b in range(PACK):
        kept = jnp.where((group == b) & (member == b), turned(rows, b - slice_index), kept)
    return jnp.concatenate(
        [jnp.sum(kept[a * PACK : (a + 1) * PACK], axis=0, keepdims=True) for a in range(2)], axis=0
    )


def power_kernel(parts_ref, d_ref, c_ref, a_ref, b_ref, out_ref):
    channels = parts_ref.shape[0]
    rows = a_ref.shape[0] - COUNT_ROWS
    slices = channels // SLICE
    cosines = parts_ref[:, :channels]
    sines = parts_ref[:, channels:]

    def dot(x, y):
        return jnp.dot(x, y, preferred_element_type=jnp.float32)

    def delays(ref):
        re, im = ref[:rows, :channels], ref[:rows, channels:]
        return dot(re, cosines) + dot(im, sines), dot(im, cosines) - dot(re, sines)

    blocks = [delays(ref) for ref in (a_ref, b_ref, c_ref, d_ref)]
    pairs = pair_sum(*(re for re, _ in blocks)) + pair_sum(*(im for _, im in blocks))
    power = jnp.sum(pairs.reshape(rows // GR_DEV, GR_DEV, channels), axis=0)
    counts = [ref[rows:, :LANES].astype(jnp.float32)[:GR_DEV] for ref in (a_ref, b_ref, c_ref, d_ref)]
    count = jnp.sum(pair_sum(*counts), axis=1, keepdims=True)
    count = packed(jnp.broadcast_to(count, (GR_DEV, LANES)), 0)
    for j in range(slices):
        half = power[:, j // PACK * LANES : (j // PACK + 1) * LANES]
        chunk = jnp.concatenate([packed(half, j % PACK), count], axis=0)
        for copy in range(out_ref.shape[0] // slices):
            out_ref[copy * slices + j] = chunk


def choose_kernel(times, spot_ref, in_ref, out_ref):
    spectrum = []
    for z in range(in_ref.shape[0] // times):
        total = in_ref[z * times]
        for time in range(1, times):
            total = total + in_ref[z * times + time]
        spectrum.append(total[:2] / jnp.maximum(total[2:], 1.0))
    spectrum = jnp.concatenate(spectrum, axis=0)
    first = lane_group(spectrum.shape) == 0
    rows = jnp.concatenate([jnp.where(first, turned(spectrum, -b), 0.0) for b in range(PACK)], axis=0)
    column = lax.broadcasted_iota(jnp.int32, (spot_ref.shape[0], rows.shape[0]), 1)
    pick = (spot_ref[...] == column).astype(jnp.float32)
    chosen = exact_dot(pick, rows)
    size = chosen.shape[0] // PACK
    chunks = turned(chosen[:size], 0)
    for b in range(1, PACK):
        chunks = chunks + turned(chosen[b * size : (b + 1) * size], b)
    copies = out_ref.shape[0] // (size // 2)
    for y in range(size // 2):
        for copy in range(copies):
            out_ref[y * copies + copy] = chunks[2 * y : 2 * y + 2]


def unpack_kernel(in_ref, out_ref):
    slices = out_ref.shape[1] // SLICE
    group = lane_group((GR_DEV, LANES))
    member = lax.broadcasted_iota(jnp.int32, (GR_DEV, LANES), 0) % PACK
    for half in range(slices // PACK):
        result = jnp.zeros((GR_DEV, LANES), jnp.float32)
        for k in range(PACK):
            j = half * PACK + k
            total = in_ref[j]
            for y in range(1, in_ref.shape[0] // slices):
                total = total + in_ref[y * slices + j]
            total = jnp.concatenate(
                [jnp.broadcast_to(total[a : a + 1], (PACK, LANES)) for a in range(2)], axis=0
            )
            for b in range(PACK):
                result = jnp.where((group == k) & (member == b), turned(total, k - b), result)
        out_ref[:, half * LANES : (half + 1) * LANES] = result


def small_call(kernel, shape, name):
    return pl.pallas_call(
        kernel,
        out_shape=jax.ShapeDtypeStruct(shape, jnp.float32),
        compiler_params=pltpu.CompilerParams(vmem_limit_bytes=16 << 20),
        name=name,
    )


def on_device(visibilities, flags, group_ids, group_order, taper, inv_cov):
    channels = taper.shape[0]
    y_size, z_size, times = (lax.axis_size(axis) for axis in ("y", "z", "ta"))
    block_total = y_size * z_size
    slices = channels // SLICE

    place = lax.axis_index(BLOCK_AXES)[None]
    blocks = group_sums(visibilities, flags, group_ids, place, block_total)
    blocks = [shifted(block, by) if by else block for block, by in zip(blocks, (-2, -1, 1, 0))]
    parts = transform_parts(taper, inv_cov)

    order = group_order.reshape(y_size, z_size, 2, PACK)
    wanted = lax.dynamic_index_in_dim(order, lax.axis_index("z"), 1, keepdims=False)
    wanted = wanted.transpose(2, 0, 1).reshape(-1, 1)
    holder = (wanted // GR_DEV + 1) % block_total
    member = wanted % GR_DEV
    spot = (member % PACK * z_size + holder % z_size) * 2 + member // PACK
    spot = jnp.where(holder // z_size == lax.axis_index("y"), spot, -1)
    parts, spot = lax.optimization_barrier((parts, spot))

    power = small_call(power_kernel, (z_size * slices, 4, LANES), "power_rows")(parts, *blocks)
    choose = functools.partial(choose_kernel, times)
    chosen = small_call(choose, (y_size * times, 2, LANES), "choose_rows")(spot, exchange(power, ("z", "ta")))

    found = exchange(chosen, ("y", "ta"))
    return small_call(unpack_kernel, (GR_DEV, channels), "unpack_rows")(found)


def solution(mesh):
    blocks, times = mesh.devices.shape
    y_size = 2 ** (int(math.log2(blocks)) // 2)
    cut = Mesh(mesh.devices.reshape(y_size, blocks // y_size, times), ("y", "z", "ta"))
    return jax.shard_map(
        on_device,
        mesh=cut,
        in_specs=(P("ta", BLOCK_AXES, None), P("ta", BLOCK_AXES), P(BLOCK_AXES), P(), P(), P()),
        out_specs=P(BLOCK_AXES, None),
        check_vma=False,
    )
```

```python
import functools
import math

import numpy as np
import jax
import jax.numpy as jnp
from jax import lax
from jax.experimental import pallas as pl
from jax.experimental.pallas import tpu as pltpu
from jax.sharding import Mesh
from jax.sharding import PartitionSpec as P

GR_DEV = 8
SPAN = 4
LANES = 128
BLOCK_AXES = ("y", "z")
TIME_AXES = ("x", "core")
COUNT_ROWS = 16
SLICE = 64
TOGETHER = 8


def shifted(shard, by):
    devices = lax.axis_size(BLOCK_AXES)
    return lax.ppermute(shard, BLOCK_AXES, [(i, (i + by) % devices) for i in range(devices)])


def exchange(chunks, axis):
    return lax.all_to_all(chunks, axis, 0, 0, tiled=True)


def fourier_table(channels):
    ramp = np.arange(channels)
    angles = 2.0 * math.pi / channels * (ramp[:, None] * ramp[None, :] % channels)
    both = np.concatenate([np.cos(angles), np.sin(angles)], axis=1) / math.sqrt(channels)
    return both.astype(np.float32)


def exact_dot(x, y):
    return jnp.dot(x, y, precision=lax.Precision.HIGHEST, preferred_element_type=jnp.float32)


def transform_parts(taper, inv_cov):
    weighted = taper[:, None] * inv_cov
    return exact_dot(weighted, jnp.asarray(fourier_table(taper.shape[0]))).astype(jnp.bfloat16)


BLOCK_STEPS = (3, 2, 0, 1)


def group_kernel(block_total, place_ref, ids_hbm, flags_hbm, vis_hbm, *rest):
    *refs, ids_ref, flags_ref, held_ref, few_sems, sems = rest
    time_count, _, row_width = vis_hbm.shape
    few = [
        pltpu.make_async_copy(source, target, few_sems.at[i])
        for i, (source, target) in enumerate(((ids_hbm, ids_ref), (flags_hbm, flags_ref)))
    ]
    copies = [pltpu.make_async_copy(vis_hbm.at[t], held_ref.at[t], sems.at[t]) for t in range(time_count)]
    for copy in few + copies:
        copy.start()
    for copy in few:
        copy.wait()
    ids = ids_ref[...]
    back = place_ref[0] - (ids >> 3)
    back = jnp.where(back < 0, back + block_total, back)
    row = lax.broadcasted_iota(jnp.int32, (SPAN * GR_DEV, ids.shape[1]), 0)
    onehot = (row == back * GR_DEV + (ids & (GR_DEV - 1))).astype(jnp.float32)
    lane = lax.broadcasted_iota(jnp.int32, (SPAN * GR_DEV, LANES), 1)
    counts = jnp.zeros((SPAN * GR_DEV, LANES), jnp.float32)
    for first in range(0, time_count, TOGETHER):
        tables = []
        for t in range(first, first + TOGETHER):
            table = onehot * flags_ref[t : t + 1, :].astype(jnp.float32)
            counts = jnp.where(lane == t, jnp.sum(table, axis=1, keepdims=True), counts)
            tables.append(table.astype(jnp.bfloat16))
        for t in range(first, first + TOGETHER):
            copies[t].wait()
        sums = [
            jnp.dot(table, held_ref[first + i], preferred_element_type=jnp.float32)
            for i, table in enumerate(tables)
        ]
        for step, ref in zip(BLOCK_STEPS, refs):
            span = slice(step * GR_DEV, (step + 1) * GR_DEV)
            both = jnp.concatenate([one[span] for one in sums], axis=0)
            ref[first * GR_DEV : (first + TOGETHER) * GR_DEV, :] = both.astype(jnp.bfloat16)
    for step, ref in zip(BLOCK_STEPS, refs):
        mine = counts[step * GR_DEV : (step + 1) * GR_DEV]
        tile = jnp.concatenate([mine, jnp.zeros_like(mine)], axis=0)
        tile = jnp.concatenate([tile, jnp.zeros((COUNT_ROWS, row_width - LANES), jnp.float32)], axis=1)
        ref[time_count * GR_DEV :, :] = tile.astype(jnp.bfloat16)


def group_sums(visibilities, flags, group_ids, place, block_total):
    time_count, block_length, row_width = visibilities.shape
    block = pltpu.VMEM((time_count * GR_DEV + COUNT_ROWS, row_width), jnp.bfloat16)
    arrays = [pltpu.with_memory_space_constraint(x, pltpu.HBM) for x in (group_ids[None, :], flags, visibilities)]
    return pl.pallas_call(
        functools.partial(group_kernel, block_total),
        in_specs=[pl.BlockSpec(memory_space=pltpu.SMEM)] + [pl.BlockSpec(memory_space=pltpu.HBM)] * len(arrays),
        out_specs=[pl.BlockSpec(memory_space=pltpu.VMEM)] * SPAN,
        out_shape=[block] * SPAN,
        scratch_shapes=[pltpu.VMEM(x.shape, x.dtype) for x in arrays]
        + [pltpu.SemaphoreType.DMA((2,)), pltpu.SemaphoreType.DMA((time_count,))],
        compiler_params=pltpu.CompilerParams(vmem_limit_bytes=16 << 20),
        cost_estimate=pl.CostEstimate(
            flops=2 * time_count * SPAN * GR_DEV * block_length * row_width,
            bytes_accessed=visibilities.size * 2,
            transcendentals=0,
        ),
        name="group_sums",
    )(place, *arrays)


def pair_sum(a, b, c, d):
    return b * a + c * (a + b) + d * (a + b + c)


def power_kernel(parts_ref, d_ref, c_ref, a_ref, b_ref, out_ref):
    channels = parts_ref.shape[0]
    rows = a_ref.shape[0] - COUNT_ROWS
    slices = channels // SLICE
    cosines = parts_ref[:, :channels]
    sines = parts_ref[:, channels:]

    def dot(x, y):
        return jnp.dot(x, y, preferred_element_type=jnp.float32)

    def delays(ref):
        re, im = ref[:rows, :channels], ref[:rows, channels:]
        return dot(re, cosines) + dot(im, sines), dot(im, cosines) - dot(re, sines)

    blocks = [delays(ref) for ref in (a_ref, b_ref, c_ref, d_ref)]
    pairs = pair_sum(*(re for re, _ in blocks)) + pair_sum(*(im for _, im in blocks))
    power = jnp.sum(pairs.reshape(rows // GR_DEV, GR_DEV, channels), axis=0)
    counts = [ref[rows:, :LANES].astype(jnp.float32)[:GR_DEV] for ref in (a_ref, b_ref, c_ref, d_ref)]
    count = jnp.sum(pair_sum(*counts), axis=1, keepdims=True)
    count = jnp.broadcast_to(count, (GR_DEV, LANES))
    low = lax.broadcasted_iota(jnp.int32, (GR_DEV, LANES), 1) < SLICE
    for j in range(slices):
        lanes = power[:, j * SLICE // LANES * LANES :][:, :LANES]
        if j % 2:
            lanes = pltpu.roll(lanes, SLICE, 1)
        chunk = jnp.where(low, lanes, count)
        for copy in range(out_ref.shape[0] // slices):
            out_ref[copy * slices + j] = chunk


def choose_kernel(slices, spot_ref, in_ref, out_ref):
    rows = []
    for z in range(in_ref.shape[0] // slices):
        total = in_ref[z * slices]
        for x in range(1, slices):
            total = total + in_ref[z * slices + x]
        rows.append(total)
    rows = jnp.concatenate(rows, axis=0)
    column = lax.broadcasted_iota(jnp.int32, (spot_ref.shape[0], rows.shape[0]), 1)
    chosen = exact_dot((spot_ref[...] == column).astype(jnp.float32), rows)
    for y in range(out_ref.shape[0] // slices):
        for copy in range(slices):
            out_ref[y * slices + copy] = chosen[y * GR_DEV : (y + 1) * GR_DEV]


def join_kernel(slices, in_ref, out_ref):
    low = lax.broadcasted_iota(jnp.int32, (GR_DEV, LANES), 1) < SLICE
    totals = []
    for x in range(slices):
        total = in_ref[x]
        for y in range(1, in_ref.shape[0] // slices):
            total = total + in_ref[y * slices + x]
        totals.append(total)
    for pair in range(slices // 2):
        after = pltpu.roll(totals[2 * pair + 1], SLICE, 1)
        out_ref[:, pair * LANES : (pair + 1) * LANES] = jnp.where(low, totals[2 * pair], after)
    out_ref[:, slices // 2 * LANES :] = jnp.where(low, pltpu.roll(totals[0], SLICE, 1), totals[0])


def small_call(kernel, shape, name):
    return pl.pallas_call(
        kernel,
        out_shape=jax.ShapeDtypeStruct(shape, jnp.float32),
        compiler_params=pltpu.CompilerParams(vmem_limit_bytes=16 << 20),
        name=name,
    )


def on_device(visibilities, flags, group_ids, group_order, taper, inv_cov):
    channels = taper.shape[0]
    y_size, z_size, slices = (lax.axis_size(axis) for axis in ("y", "z", "x"))
    block_total = y_size * z_size

    place = lax.axis_index(BLOCK_AXES)[None]
    blocks = group_sums(visibilities, flags, group_ids, place, block_total)
    blocks = [shifted(block, by) if by else block for block, by in zip(blocks, (-2, -1, 1, 0))]
    parts = transform_parts(taper, inv_cov)

    order = group_order.reshape(y_size, z_size, GR_DEV)
    wanted = lax.dynamic_index_in_dim(order, lax.axis_index("z"), 1, keepdims=False).reshape(-1, 1)
    holder = (wanted // GR_DEV + 1) % block_total
    spot = holder % z_size * GR_DEV + wanted % GR_DEV
    spot = jnp.where(holder // z_size == lax.axis_index("y"), spot, -1)
    parts, spot = lax.optimization_barrier((parts, spot))

    power = small_call(power_kernel, (z_size * slices, GR_DEV, LANES), "power_rows")(parts, *blocks)
    choose = functools.partial(choose_kernel, slices)
    shape = (y_size * slices, GR_DEV, LANES)
    chosen = small_call(choose, shape, "choose_rows")(spot, exchange(power, ("z", "x")))

    join = functools.partial(join_kernel, slices)
    found = exchange(chosen, ("y", "x"))
    partial = small_call(join, (GR_DEV, channels + LANES), "join_slices")(found)

    totals = partial + lax.ppermute(partial, "core", [(0, 1), (1, 0)])
    return totals[:, :channels] / jnp.maximum(totals[:, channels : channels + 1], 1.0)


def solution(mesh):
    blocks, times = mesh.devices.shape
    y_size = 2 ** (int(math.log2(blocks)) // 2)
    cut = Mesh(
        mesh.devices.reshape(y_size, blocks // y_size, times // 2, 2), ("y", "z", "x", "core")
    )
    return jax.shard_map(
        on_device,
        mesh=cut,
        in_specs=(P(TIME_AXES, BLOCK_AXES, None), P(TIME_AXES, BLOCK_AXES), P(BLOCK_AXES), P(), P(), P()),
        out_specs=P(BLOCK_AXES, None),
        check_vma=False,
    )
```

```python
import functools
import math

import numpy as np
import jax
import jax.numpy as jnp
from jax import lax
from jax.experimental import pallas as pl
from jax.experimental.pallas import tpu as pltpu
from jax.sharding import Mesh
from jax.sharding import PartitionSpec as P

GR_DEV = 8
SPAN = 4
LANES = 128
BLOCK_AXES = ("y", "z")
TIME_AXES = ("x", "core")
COUNT_ROWS = 16
SLICE = 64
TOGETHER = 8


def opposed(shard, by):
    blocks = lax.axis_size(BLOCK_AXES)
    times = lax.axis_size(TIME_AXES)
    pairs = []
    for block in range(blocks):
        for time in range(times):
            target = (block + (by if time % 2 else -by)) % blocks
            pairs.append((block * times + time, target * times + time))
    return lax.ppermute(shard, (*BLOCK_AXES, *TIME_AXES), pairs)


def exchange(chunks, axis):
    return lax.all_to_all(chunks, axis, 0, 0, tiled=True)


def fourier_table(channels):
    ramp = np.arange(channels)
    angles = 2.0 * math.pi / channels * (ramp[:, None] * ramp[None, :] % channels)
    both = np.concatenate([np.cos(angles), np.sin(angles)], axis=1) / math.sqrt(channels)
    return both.astype(np.float32)


def exact_dot(x, y):
    return jnp.dot(x, y, precision=lax.Precision.HIGHEST, preferred_element_type=jnp.float32)


def transform_parts(taper, inv_cov):
    weighted = taper[:, None] * inv_cov
    return exact_dot(weighted, jnp.asarray(fourier_table(taper.shape[0]))).astype(jnp.bfloat16)


BLOCK_STEPS = (3, 2, 0, 1)


def group_kernel(block_total, place_ref, ids_hbm, flags_hbm, vis_hbm, *rest):
    *refs, ids_ref, flags_ref, held_ref, few_sems, sems = rest
    time_count, _, row_width = vis_hbm.shape
    few = [
        pltpu.make_async_copy(source, target, few_sems.at[i])
        for i, (source, target) in enumerate(((ids_hbm, ids_ref), (flags_hbm, flags_ref)))
    ]
    copies = [pltpu.make_async_copy(vis_hbm.at[t], held_ref.at[t], sems.at[t]) for t in range(time_count)]
    for copy in few + copies:
        copy.start()
    for copy in few:
        copy.wait()
    ids = ids_ref[...]
    back = place_ref[0] - (ids >> 3)
    back = jnp.where(back < 0, back + block_total, back)
    back = jnp.where(place_ref[1] == 0, SPAN - 1 - back, back)
    row = lax.broadcasted_iota(jnp.int32, (SPAN * GR_DEV, ids.shape[1]), 0)
    onehot = (row == back * GR_DEV + (ids & (GR_DEV - 1))).astype(jnp.float32)
    lane = lax.broadcasted_iota(jnp.int32, (SPAN * GR_DEV, LANES), 1)
    counts = jnp.zeros((SPAN * GR_DEV, LANES), jnp.float32)
    for first in range(0, time_count, TOGETHER):
        tables = []
        for t in range(first, first + TOGETHER):
            table = onehot * flags_ref[t : t + 1, :].astype(jnp.float32)
            counts = jnp.where(lane == t, jnp.sum(table, axis=1, keepdims=True), counts)
            tables.append(table.astype(jnp.bfloat16))
        for t in range(first, first + TOGETHER):
            copies[t].wait()
        sums = [
            jnp.dot(table, held_ref[first + i], preferred_element_type=jnp.float32)
            for i, table in enumerate(tables)
        ]
        for step, ref in zip(BLOCK_STEPS, refs):
            span = slice(step * GR_DEV, (step + 1) * GR_DEV)
            both = jnp.concatenate([one[span] for one in sums], axis=0)
            ref[first * GR_DEV : (first + TOGETHER) * GR_DEV, :] = both.astype(jnp.bfloat16)
    for step, ref in zip(BLOCK_STEPS, refs):
        mine = counts[step * GR_DEV : (step + 1) * GR_DEV]
        tile = jnp.concatenate([mine, jnp.zeros_like(mine)], axis=0)
        tile = jnp.concatenate([tile, jnp.zeros((COUNT_ROWS, row_width - LANES), jnp.float32)], axis=1)
        ref[time_count * GR_DEV :, :] = tile.astype(jnp.bfloat16)


def group_sums(visibilities, flags, group_ids, place, block_total):
    time_count, block_length, row_width = visibilities.shape
    block = pltpu.VMEM((time_count * GR_DEV + COUNT_ROWS, row_width), jnp.bfloat16)
    arrays = [pltpu.with_memory_space_constraint(x, pltpu.HBM) for x in (group_ids[None, :], flags, visibilities)]
    return pl.pallas_call(
        functools.partial(group_kernel, block_total),
        in_specs=[pl.BlockSpec(memory_space=pltpu.SMEM)] + [pl.BlockSpec(memory_space=pltpu.HBM)] * len(arrays),
        out_specs=[pl.BlockSpec(memory_space=pltpu.VMEM)] * SPAN,
        out_shape=[block] * SPAN,
        scratch_shapes=[pltpu.VMEM(x.shape, x.dtype) for x in arrays]
        + [pltpu.SemaphoreType.DMA((2,)), pltpu.SemaphoreType.DMA((time_count,))],
        compiler_params=pltpu.CompilerParams(vmem_limit_bytes=16 << 20),
        cost_estimate=pl.CostEstimate(
            flops=2 * time_count * SPAN * GR_DEV * block_length * row_width,
            bytes_accessed=visibilities.size * 2,
            transcendentals=0,
        ),
        name="group_sums",
    )(place, *arrays)


def pair_sum(a, b, c, d):
    return b * a + c * (a + b) + d * (a + b + c)


def power_kernel(parts_ref, d_ref, c_ref, a_ref, b_ref, out_ref):
    channels = parts_ref.shape[0]
    rows = a_ref.shape[0] - COUNT_ROWS
    slices = channels // SLICE
    cosines = parts_ref[:, :channels]
    sines = parts_ref[:, channels:]

    def dot(x, y):
        return jnp.dot(x, y, preferred_element_type=jnp.float32)

    def delays(ref):
        re, im = ref[:rows, :channels], ref[:rows, channels:]
        return dot(re, cosines) + dot(im, sines), dot(im, cosines) - dot(re, sines)

    blocks = [delays(ref) for ref in (a_ref, b_ref, c_ref, d_ref)]
    pairs = pair_sum(*(re for re, _ in blocks)) + pair_sum(*(im for _, im in blocks))
    power = jnp.sum(pairs.reshape(rows // GR_DEV, GR_DEV, channels), axis=0)
    counts = [ref[rows:, :LANES].astype(jnp.float32)[:GR_DEV] for ref in (a_ref, b_ref, c_ref, d_ref)]
    count = jnp.sum(pair_sum(*counts), axis=1, keepdims=True)
    count = pack_counts(count)
    low = low_lanes(1)
    for j in range(slices):
        lanes = power[:, j * SLICE // LANES * LANES :][:, :LANES]
        turned = pltpu.roll(lanes, SLICE, 1)
        first, second = (turned, lanes) if j % 2 else (lanes, turned)
        for copy in range(out_ref.shape[0] // slices):
            store_chunk(out_ref, copy * slices + j, first, second, count)


def low_lanes(rows):
    return lax.broadcasted_iota(jnp.int32, (rows, LANES), 1) < SLICE


def count_lanes(rows):
    lane = lax.broadcasted_iota(jnp.int32, (rows, LANES), 1)
    return lane == lax.broadcasted_iota(jnp.int32, (rows, LANES), 0) % GR_DEV * (LANES // GR_DEV)


def pack_counts(count):
    return jnp.sum(jnp.where(count_lanes(GR_DEV), count, 0.0), axis=0, keepdims=True)


def store_chunk(out_ref, index, first, second, count):
    low = low_lanes(1)
    for i in range(GR_DEV // 2):
        row = jnp.where(low, first[2 * i : 2 * i + 1], second[2 * i + 1 : 2 * i + 2])
        out_ref[index, :, i * LANES : (i + 1) * LANES] = row
    out_ref[index, :, GR_DEV // 2 * LANES :] = count


def choose_kernel(slices, spot_ref, in_ref, out_ref):
    planes = []
    for z in range(in_ref.shape[0] // slices):
        total = in_ref[z * slices]
        for x in range(1, slices):
            total = total + in_ref[z * slices + x]
        planes.append(total)
    planes = jnp.concatenate(planes, axis=0)
    spot = spot_ref[...]
    member = spot & (GR_DEV - 1)
    column = lax.broadcasted_iota(jnp.int32, (spot.shape[0], planes.shape[0]), 1)
    found = exact_dot((spot >> 3 == column).astype(jnp.float32), planes)
    lanes = jnp.zeros((spot.shape[0], LANES), jnp.float32)
    for i in range(GR_DEV // 2):
        lanes = jnp.where(member >> 1 == i, found[:, i * LANES : (i + 1) * LANES], lanes)
    turned = pltpu.roll(lanes, SLICE, 1)
    first = jnp.where(member & 1 == 0, lanes, turned)
    second = jnp.where(member & 1 == 0, turned, lanes)
    lane = lax.broadcasted_iota(jnp.int32, lanes.shape, 1)
    count = jnp.where(lane == member * (LANES // GR_DEV), found[:, GR_DEV // 2 * LANES :], 0.0)
    count = jnp.sum(count, axis=1, keepdims=True)
    for y in range(out_ref.shape[0] // slices):
        rows = slice(y * GR_DEV, (y + 1) * GR_DEV)
        packed = pack_counts(count[rows])
        for copy in range(slices):
            store_chunk(out_ref, y * slices + copy, first[rows], second[rows], packed)


def join_kernel(slices, in_ref, out_ref):
    totals = []
    for x in range(slices):
        total = in_ref[x]
        for y in range(1, in_ref.shape[0] // slices):
            total = total + in_ref[y * slices + x]
        totals.append(total)
    low = low_lanes(1)
    for pair in range(slices // 2):
        rows = []
        for i in range(GR_DEV // 2):
            left, right = (totals[2 * pair + k][:, i * LANES : (i + 1) * LANES] for k in range(2))
            rows.append(jnp.where(low, left, pltpu.roll(right, SLICE, 1)))
            rows.append(jnp.where(low, pltpu.roll(left, SLICE, 1), right))
        out_ref[:, pair * LANES : (pair + 1) * LANES] = jnp.concatenate(rows, axis=0)
    count = jnp.broadcast_to(totals[0][:, GR_DEV // 2 * LANES :], (GR_DEV, LANES))
    count = jnp.sum(jnp.where(count_lanes(GR_DEV), count, 0.0), axis=1, keepdims=True)
    out_ref[:, slices // 2 * LANES :] = jnp.broadcast_to(count, (GR_DEV, LANES))


def small_call(kernel, shape, name):
    return pl.pallas_call(
        kernel,
        out_shape=jax.ShapeDtypeStruct(shape, jnp.float32),
        compiler_params=pltpu.CompilerParams(vmem_limit_bytes=16 << 20),
        name=name,
    )


def on_device(visibilities, flags, group_ids, group_order, taper, inv_cov):
    channels = taper.shape[0]
    y_size, z_size, slices = (lax.axis_size(axis) for axis in ("y", "z", "x"))
    block_total = y_size * z_size
    width = GR_DEV * SLICE + LANES

    core = lax.axis_index("core")
    place = jnp.stack([lax.axis_index(BLOCK_AXES), core])
    blocks = group_sums(visibilities, flags, group_ids, place, block_total)
    blocks = [opposed(block, by) if by else block for block, by in zip(blocks, (-2, -1, 1, 0))]
    parts = transform_parts(taper, inv_cov)

    order = group_order.reshape(y_size, z_size, GR_DEV)
    wanted = lax.dynamic_index_in_dim(order, lax.axis_index("z"), 1, keepdims=False).reshape(-1, 1)
    holder = (wanted // GR_DEV + 2 - core) % block_total
    spot = holder % z_size * GR_DEV + wanted % GR_DEV
    spot = jnp.where(holder // z_size == lax.axis_index("y"), spot, z_size * GR_DEV)
    parts, spot = lax.optimization_barrier((parts, spot))

    power = small_call(power_kernel, (z_size * slices, 1, width), "power_rows")(parts, *blocks)
    choose = functools.partial(choose_kernel, slices)
    shape = (y_size * slices, 1, width)
    chosen = small_call(choose, shape, "choose_rows")(spot, exchange(power, ("z", "x")))

    join = functools.partial(join_kernel, slices)
    found = exchange(chosen, ("y", "x"))
    partial = small_call(join, (GR_DEV, channels + LANES), "join_slices")(found)

    totals = partial + lax.ppermute(partial, "core", [(0, 1), (1, 0)])
    return totals[:, :channels] / jnp.maximum(totals[:, channels : channels + 1], 1.0)


def solution(mesh):
    blocks, times = mesh.devices.shape
    y_size = 2 ** (int(math.log2(blocks)) // 2)
    cut = Mesh(
        mesh.devices.reshape(y_size, blocks // y_size, times // 2, 2), ("y", "z", "x", "core")
    )
    return jax.shard_map(
        on_device,
        mesh=cut,
        in_specs=(P(TIME_AXES, BLOCK_AXES, None), P(TIME_AXES, BLOCK_AXES), P(BLOCK_AXES), P(), P(), P()),
        out_specs=P(BLOCK_AXES, None),
        check_vma=False,
    )
```

```python
import functools
import math

import numpy as np
import jax
import jax.numpy as jnp
from jax import lax
from jax.experimental import pallas as pl
from jax.experimental.pallas import tpu as pltpu
from jax.sharding import Mesh
from jax.sharding import PartitionSpec as P

GR_DEV = 8
SPAN = 4
LANES = 128
BLOCK_AXES = ("y", "z")
COUNT_ROWS = 16
SLICE = 32
PACK = 4
TOGETHER = 8


def opposed(shard, by):
    blocks = lax.axis_size(BLOCK_AXES)
    times = lax.axis_size("ta")
    pairs = []
    for block in range(blocks):
        for time in range(times):
            target = (block + (by if time % 2 else -by)) % blocks
            pairs.append((block * times + time, target * times + time))
    return lax.ppermute(shard, (*BLOCK_AXES, "ta"), pairs)


def exchange(chunks, axis):
    return lax.all_to_all(chunks, axis, 0, 0, tiled=True)


def fourier_table(channels):
    ramp = np.arange(channels)
    angles = 2.0 * math.pi / channels * (ramp[:, None] * ramp[None, :] % channels)
    both = np.concatenate([np.cos(angles), np.sin(angles)], axis=1) / math.sqrt(channels)
    return both.astype(np.float32)


def exact_dot(x, y):
    return jnp.dot(x, y, precision=lax.Precision.HIGHEST, preferred_element_type=jnp.float32)


def transform_parts(taper, inv_cov):
    weighted = taper[:, None] * inv_cov
    return exact_dot(weighted, jnp.asarray(fourier_table(taper.shape[0]))).astype(jnp.bfloat16)


BLOCK_STEPS = (3, 2, 0, 1)


def group_kernel(block_total, place_ref, ids_hbm, flags_hbm, vis_hbm, *rest):
    *refs, ids_ref, flags_ref, held_ref, few_sems, sems = rest
    time_count, _, row_width = vis_hbm.shape
    few = [
        pltpu.make_async_copy(source, target, few_sems.at[i])
        for i, (source, target) in enumerate(((ids_hbm, ids_ref), (flags_hbm, flags_ref)))
    ]
    copies = [pltpu.make_async_copy(vis_hbm.at[t], held_ref.at[t], sems.at[t]) for t in range(time_count)]
    for copy in few + copies:
        copy.start()
    for copy in few:
        copy.wait()
    ids = ids_ref[...]
    back = (place_ref[0] >> 1) - (ids >> 3)
    back = jnp.where(back < 0, back + block_total, back)
    back = jnp.where(place_ref[0] & 1 == 0, SPAN - 1 - back, back)
    row = lax.broadcasted_iota(jnp.int32, (SPAN * GR_DEV, ids.shape[1]), 0)
    onehot = (row == back * GR_DEV + (ids & (GR_DEV - 1))).astype(jnp.float32)
    lane = lax.broadcasted_iota(jnp.int32, (SPAN * GR_DEV, LANES), 1)
    counts = jnp.zeros((SPAN * GR_DEV, LANES), jnp.float32)
    for first in range(0, time_count, TOGETHER):
        tables = []
        for t in range(first, first + TOGETHER):
            table = onehot * flags_ref[t : t + 1, :].astype(jnp.float32)
            counts = jnp.where(lane == t, jnp.sum(table, axis=1, keepdims=True), counts)
            tables.append(table.astype(jnp.bfloat16))
        for t in range(first, first + TOGETHER):
            copies[t].wait()
        sums = [
            jnp.dot(table, held_ref[first + i], preferred_element_type=jnp.float32)
            for i, table in enumerate(tables)
        ]
        for step, ref in zip(BLOCK_STEPS, refs):
            span = slice(step * GR_DEV, (step + 1) * GR_DEV)
            both = jnp.concatenate([one[span] for one in sums], axis=0)
            ref[first * GR_DEV : (first + TOGETHER) * GR_DEV, :] = both.astype(jnp.bfloat16)
    for step, ref in zip(BLOCK_STEPS, refs):
        mine = counts[step * GR_DEV : (step + 1) * GR_DEV]
        tile = jnp.concatenate([mine, jnp.zeros_like(mine)], axis=0)
        tile = jnp.concatenate([tile, jnp.zeros((COUNT_ROWS, row_width - LANES), jnp.float32)], axis=1)
        ref[time_count * GR_DEV :, :] = tile.astype(jnp.bfloat16)


def group_sums(visibilities, flags, group_ids, place, block_total):
    time_count, block_length, row_width = visibilities.shape
    block = pltpu.VMEM((time_count * GR_DEV + COUNT_ROWS, row_width), jnp.bfloat16)
    arrays = [pltpu.with_memory_space_constraint(x, pltpu.HBM) for x in (group_ids[None, :], flags, visibilities)]
    return pl.pallas_call(
        functools.partial(group_kernel, block_total),
        in_specs=[pl.BlockSpec(memory_space=pltpu.SMEM)] + [pl.BlockSpec(memory_space=pltpu.HBM)] * len(arrays),
        out_specs=[pl.BlockSpec(memory_space=pltpu.VMEM)] * SPAN,
        out_shape=[block] * SPAN,
        scratch_shapes=[pltpu.VMEM(x.shape, x.dtype) for x in arrays]
        + [pltpu.SemaphoreType.DMA((2,)), pltpu.SemaphoreType.DMA((time_count,))],
        compiler_params=pltpu.CompilerParams(vmem_limit_bytes=16 << 20),
        cost_estimate=pl.CostEstimate(
            flops=2 * time_count * SPAN * GR_DEV * block_length * row_width,
            bytes_accessed=visibilities.size * 2,
            transcendentals=0,
        ),
        name="group_sums",
    )(place, *arrays)


def pair_sum(a, b, c, d):
    return b * a + c * (a + b) + d * (a + b + c)


def lane_group(shape):
    return lax.broadcasted_iota(jnp.int32, shape, len(shape) - 1) // SLICE


def turned(rows, groups):
    return pltpu.roll(rows, groups % PACK * SLICE, 1) if groups % PACK else rows


def packed(rows, slice_index):
    group = lane_group(rows.shape)
    member = lax.broadcasted_iota(jnp.int32, rows.shape, 0) % PACK
    kept = jnp.zeros_like(rows)
    for b in range(PACK):
        kept = jnp.where((group == b) & (member == b), turned(rows, b - slice_index), kept)
    return jnp.concatenate(
        [jnp.sum(kept[a * PACK : (a + 1) * PACK], axis=0, keepdims=True) for a in range(2)], axis=0
    )


def power_kernel(parts_ref, d_ref, c_ref, a_ref, b_ref, out_ref):
    channels = parts_ref.shape[0]
    rows = a_ref.shape[0] - COUNT_ROWS
    slices = channels // SLICE
    cosines = parts_ref[:, :channels]
    sines = parts_ref[:, channels:]

    def dot(x, y):
        return jnp.dot(x, y, preferred_element_type=jnp.float32)

    def delays(ref):
        re, im = ref[:rows, :channels], ref[:rows, channels:]
        return dot(re, cosines) + dot(im, sines), dot(im, cosines) - dot(re, sines)

    blocks = [delays(ref) for ref in (a_ref, b_ref, c_ref, d_ref)]
    pairs = pair_sum(*(re for re, _ in blocks)) + pair_sum(*(im for _, im in blocks))
    power = jnp.sum(pairs.reshape(rows // GR_DEV, GR_DEV, channels), axis=0)
    counts = [ref[rows:, :LANES].astype(jnp.float32)[:GR_DEV] for ref in (a_ref, b_ref, c_ref, d_ref)]
    count = jnp.sum(pair_sum(*counts), axis=1, keepdims=True)
    count = pack_counts(count)
    for j in range(slices):
        half = power[:, j // PACK * LANES : (j // PACK + 1) * LANES]
        chunk = packed(half, j % PACK)
        for copy in range(out_ref.shape[0] // slices):
            store_chunk(out_ref, copy * slices + j, chunk, count)


def count_lanes(rows):
    lane = lax.broadcasted_iota(jnp.int32, (rows, LANES), 1)
    return lane == lax.broadcasted_iota(jnp.int32, (rows, LANES), 0) % GR_DEV * (LANES // GR_DEV)


def pack_counts(count):
    return jnp.sum(jnp.where(count_lanes(GR_DEV), count, 0.0), axis=0, keepdims=True)


def store_chunk(out_ref, index, rows, count):
    out_ref[index, :, :LANES] = rows[:1]
    out_ref[index, :, LANES : 2 * LANES] = rows[1:]
    out_ref[index, :, 2 * LANES :] = count


def choose_kernel(times, spot_ref, in_ref, out_ref):
    planes = []
    for core in range(2):
        for z in range(in_ref.shape[0] // times):
            total = in_ref[z * times + core]
            for time in range(core + 2, times, 2):
                total = total + in_ref[z * times + time]
            planes.append(total)
    planes = jnp.concatenate(planes, axis=0)
    member = spot_ref[:, 2:3]
    column = lax.broadcasted_iota(jnp.int32, (member.shape[0], planes.shape[0]), 1)
    pick = (spot_ref[:, 0:1] == column) | (spot_ref[:, 1:2] == column)
    found = exact_dot(pick.astype(jnp.float32), planes)
    lanes = jnp.where(member < PACK, found[:, :LANES], found[:, LANES : 2 * LANES])
    rows = lanes
    for b in range(1, PACK):
        rows = jnp.where(member % PACK == b, turned(lanes, -b), rows)
    lane = lax.broadcasted_iota(jnp.int32, rows.shape, 1)
    count = jnp.where(lane == member * (LANES // GR_DEV), found[:, 2 * LANES :], 0.0)
    count = jnp.sum(count, axis=1, keepdims=True)
    copies = times
    for y in range(out_ref.shape[0] // copies):
        span = slice(y * GR_DEV, (y + 1) * GR_DEV)
        chunk, counts = packed(rows[span], 0), pack_counts(count[span])
        for copy in range(copies):
            store_chunk(out_ref, y * copies + copy, chunk, counts)


def unpack_kernel(in_ref, out_ref):
    slices = out_ref.shape[1] // SLICE
    group = lane_group((GR_DEV, LANES))
    member = lax.broadcasted_iota(jnp.int32, (GR_DEV, LANES), 0) % PACK
    totals = []
    for j in range(slices):
        total = in_ref[j]
        for y in range(1, in_ref.shape[0] // slices):
            total = total + in_ref[y * slices + j]
        totals.append(total)
    count = jnp.where(count_lanes(GR_DEV), jnp.broadcast_to(totals[0][:, 2 * LANES :], (GR_DEV, LANES)), 0.0)
    count = jnp.maximum(jnp.sum(count, axis=1, keepdims=True), 1.0)
    for half in range(slices // PACK):
        result = jnp.zeros((GR_DEV, LANES), jnp.float32)
        for k in range(PACK):
            total = totals[half * PACK + k]
            rows = jnp.concatenate(
                [jnp.broadcast_to(total[:, a * LANES : (a + 1) * LANES], (PACK, LANES)) for a in range(2)], axis=0
            )
            for b in range(PACK):
                result = jnp.where((group == k) & (member == b), turned(rows, k - b), result)
        out_ref[:, half * LANES : (half + 1) * LANES] = result / count


def small_call(kernel, shape, name):
    return pl.pallas_call(
        kernel,
        out_shape=jax.ShapeDtypeStruct(shape, jnp.float32),
        compiler_params=pltpu.CompilerParams(vmem_limit_bytes=16 << 20),
        name=name,
    )


def on_device(visibilities, flags, group_ids, group_order, taper, inv_cov):
    channels = taper.shape[0]
    y_size, z_size, times = (lax.axis_size(axis) for axis in ("y", "z", "ta"))
    block_total = y_size * z_size
    slices = channels // SLICE
    width = GR_DEV * SLICE + LANES

    place = (lax.axis_index(BLOCK_AXES) * 2 + lax.axis_index("ta") % 2)[None]
    blocks = group_sums(visibilities, flags, group_ids, place, block_total)
    blocks = [opposed(block, by) if by else block for block, by in zip(blocks, (-2, -1, 1, 0))]
    parts = transform_parts(taper, inv_cov)

    order = group_order.reshape(y_size, z_size, GR_DEV)
    wanted = lax.dynamic_index_in_dim(order, lax.axis_index("z"), 1, keepdims=False).reshape(-1)
    columns = []
    for core in range(2):
        holder = (wanted // GR_DEV + 2 - core) % block_total
        column = core * z_size + holder % z_size
        columns.append(jnp.where(holder // z_size == lax.axis_index("y"), column, -1))
    spot = jnp.stack([*columns, wanted % GR_DEV], axis=1)
    parts, spot = lax.optimization_barrier((parts, spot))

    power = small_call(power_kernel, (z_size * slices, 1, width), "power_rows")(parts, *blocks)
    choose = functools.partial(choose_kernel, times)
    shape = (y_size * times, 1, width)
    chosen = small_call(choose, shape, "choose_rows")(spot, exchange(power, ("z", "ta")))

    found = exchange(chosen, ("y", "ta"))
    return small_call(unpack_kernel, (GR_DEV, channels), "unpack_rows")(found)


def solution(mesh):
    blocks, times = mesh.devices.shape
    y_size = 2 ** (int(math.log2(blocks)) // 2)
    cut = Mesh(mesh.devices.reshape(y_size, blocks // y_size, times), ("y", "z", "ta"))
    return jax.shard_map(
        on_device,
        mesh=cut,
        in_specs=(P("ta", BLOCK_AXES, None), P("ta", BLOCK_AXES), P(BLOCK_AXES), P(), P(), P()),
        out_specs=P(BLOCK_AXES, None),
        check_vma=False,
    )
```

```python
import functools
import math

import numpy as np
import jax
import jax.numpy as jnp
from jax import lax
from jax.experimental import pallas as pl
from jax.experimental.pallas import tpu as pltpu
from jax.sharding import Mesh
from jax.sharding import PartitionSpec as P

GR_DEV = 8
SPAN = 4
LANES = 128
BLOCK_AXES = ("y", "z")
COUNT_ROWS = 8
SLICE = 32
PACK = 4
TOGETHER = 16


def opposed(shard, by):
    blocks = lax.axis_size(BLOCK_AXES)
    times = lax.axis_size("ta")
    pairs = []
    for block in range(blocks):
        for time in range(times):
            target = (block + (by if time % 2 else -by)) % blocks
            pairs.append((block * times + time, target * times + time))
    return lax.ppermute(shard, (*BLOCK_AXES, "ta"), pairs)


def exchange(chunks, axis):
    return lax.all_to_all(chunks, axis, 0, 0, tiled=True)


def fourier_table(channels):
    ramp = np.arange(channels)
    angles = 2.0 * math.pi / channels * (ramp[:, None] * ramp[None, :] % channels)
    both = np.concatenate([np.cos(angles), np.sin(angles)], axis=1) / math.sqrt(channels)
    return both.astype(np.float32)


def exact_dot(x, y):
    return jnp.dot(x, y, precision=lax.Precision.HIGHEST, preferred_element_type=jnp.float32)


def transform_parts(taper, inv_cov):
    weighted = taper[:, None] * inv_cov
    return exact_dot(weighted, jnp.asarray(fourier_table(taper.shape[0]))).astype(jnp.bfloat16)


BLOCK_STEPS = (3, 2, 0, 1)


def group_kernel(block_total, place_ref, ids_hbm, flags_hbm, vis_hbm, *rest):
    *refs, ids_ref, flags_ref, held_ref, few_sems, sems = rest
    time_count, _, row_width = vis_hbm.shape
    few = [
        pltpu.make_async_copy(source, target, few_sems.at[i])
        for i, (source, target) in enumerate(((ids_hbm, ids_ref), (flags_hbm, flags_ref)))
    ]
    copies = [pltpu.make_async_copy(vis_hbm.at[t], held_ref.at[t], sems.at[t]) for t in range(time_count)]
    for copy in few + copies:
        copy.start()
    for copy in few:
        copy.wait()
    ids = ids_ref[...]
    back = (place_ref[0] >> 1) - (ids >> 3)
    back = jnp.where(back < 0, back + block_total, back)
    back = jnp.where(place_ref[0] & 1 == 0, SPAN - 1 - back, back)
    row = lax.broadcasted_iota(jnp.int32, (SPAN * GR_DEV, ids.shape[1]), 0)
    onehot = (row == back * GR_DEV + (ids & (GR_DEV - 1))).astype(jnp.float32)
    lane = lax.broadcasted_iota(jnp.int32, (SPAN * GR_DEV, LANES), 1)
    counts = jnp.zeros((SPAN * GR_DEV, LANES), jnp.float32)
    for first in range(0, time_count, TOGETHER):
        tables = []
        for t in range(first, first + TOGETHER):
            table = onehot * flags_ref[t : t + 1, :].astype(jnp.float32)
            counts = jnp.where(lane == t, jnp.sum(table, axis=1, keepdims=True), counts)
            tables.append(table.astype(jnp.bfloat16))
        for t in range(first, first + TOGETHER):
            copies[t].wait()
        sums = [
            jnp.dot(table, held_ref[first + i], preferred_element_type=jnp.float32)
            for i, table in enumerate(tables)
        ]
        for step, ref in zip(BLOCK_STEPS, refs):
            span = slice(step * GR_DEV, (step + 1) * GR_DEV)
            both = jnp.concatenate([one[span] for one in sums], axis=0)
            ref[first * GR_DEV : (first + TOGETHER) * GR_DEV, :] = both.astype(jnp.bfloat16)
    for step, ref in zip(BLOCK_STEPS, refs):
        mine = counts[step * GR_DEV : (step + 1) * GR_DEV]
        tile = jnp.concatenate([mine, jnp.zeros((COUNT_ROWS, row_width - LANES), jnp.float32)], axis=1)
        ref[time_count * GR_DEV :, :] = tile.astype(jnp.bfloat16)


def group_sums(visibilities, flags, group_ids, place, block_total):
    time_count, block_length, row_width = visibilities.shape
    block = pltpu.VMEM((time_count * GR_DEV + COUNT_ROWS, row_width), jnp.bfloat16)
    arrays = [pltpu.with_memory_space_constraint(x, pltpu.HBM) for x in (group_ids[None, :], flags, visibilities)]
    return pl.pallas_call(
        functools.partial(group_kernel, block_total),
        in_specs=[pl.BlockSpec(memory_space=pltpu.SMEM)] + [pl.BlockSpec(memory_space=pltpu.HBM)] * len(arrays),
        out_specs=[pl.BlockSpec(memory_space=pltpu.VMEM)] * SPAN,
        out_shape=[block] * SPAN,
        scratch_shapes=[pltpu.VMEM(x.shape, x.dtype) for x in arrays]
        + [pltpu.SemaphoreType.DMA((2,)), pltpu.SemaphoreType.DMA((time_count,))],
        compiler_params=pltpu.CompilerParams(vmem_limit_bytes=16 << 20),
        cost_estimate=pl.CostEstimate(
            flops=2 * time_count * SPAN * GR_DEV * block_length * row_width,
            bytes_accessed=visibilities.size * 2,
            transcendentals=0,
        ),
        name="group_sums",
    )(place, *arrays)


def pair_sum(a, b, c, d):
    return b * a + c * (a + b) + d * (a + b + c)


def lane_group(shape):
    return lax.broadcasted_iota(jnp.int32, shape, len(shape) - 1) // SLICE


def turned(rows, groups):
    return pltpu.roll(rows, groups % PACK * SLICE, 1) if groups % PACK else rows


def packed(rows, slice_index):
    group = lane_group(rows.shape)
    member = lax.broadcasted_iota(jnp.int32, rows.shape, 0) % PACK
    kept = jnp.zeros_like(rows)
    for b in range(PACK):
        kept = jnp.where((group == b) & (member == b), turned(rows, b - slice_index), kept)
    return jnp.concatenate(
        [jnp.sum(kept[a * PACK : (a + 1) * PACK], axis=0, keepdims=True) for a in range(2)], axis=0
    )


def power_kernel(parts_ref, d_ref, c_ref, a_ref, b_ref, out_ref):
    channels = parts_ref.shape[0]
    rows = a_ref.shape[0] - COUNT_ROWS
    slices = channels // SLICE
    cosines = parts_ref[:, :channels]
    sines = parts_ref[:, channels:]

    def dot(x, y):
        return jnp.dot(x, y, preferred_element_type=jnp.float32)

    def delays(ref):
        re, im = ref[:rows, :channels], ref[:rows, channels:]
        return dot(re, cosines) + dot(im, sines), dot(im, cosines) - dot(re, sines)

    blocks = [delays(ref) for ref in (a_ref, b_ref, c_ref, d_ref)]
    pairs = pair_sum(*(re for re, _ in blocks)) + pair_sum(*(im for _, im in blocks))
    power = jnp.sum(pairs.reshape(rows // GR_DEV, GR_DEV, channels), axis=0)
    counts = [ref[rows:, :LANES].astype(jnp.float32) for ref in (a_ref, b_ref, c_ref, d_ref)]
    count = jnp.sum(pair_sum(*counts), axis=1, keepdims=True)
    count = pack_counts(count)
    for j in range(slices):
        half = power[:, j // PACK * LANES : (j // PACK + 1) * LANES]
        chunk = packed(half, j % PACK)
        for copy in range(out_ref.shape[0] // slices):
            store_chunk(out_ref, copy * slices + j, chunk, count)


def count_lanes(rows):
    lane = lax.broadcasted_iota(jnp.int32, (rows, LANES), 1)
    return lane == lax.broadcasted_iota(jnp.int32, (rows, LANES), 0) % GR_DEV * (LANES // GR_DEV)


def pack_counts(count):
    return jnp.sum(jnp.where(count_lanes(GR_DEV), count, 0.0), axis=0, keepdims=True)


def store_chunk(out_ref, index, rows, count):
    out_ref[index, :, :LANES] = rows[:1]
    out_ref[index, :, LANES : 2 * LANES] = rows[1:]
    out_ref[index, :, 2 * LANES :] = count


def choose_kernel(times, first_ref, second_ref, member_ref, in_ref, out_ref):
    planes = []
    for core in range(2):
        for z in range(in_ref.shape[0] // times):
            total = in_ref[z * times + core]
            for time in range(core + 2, times, 2):
                total = total + in_ref[z * times + time]
            planes.append(total)
    planes = jnp.concatenate(planes, axis=0)
    member = member_ref[...]
    column = lax.broadcasted_iota(jnp.int32, (member.shape[0], planes.shape[0]), 1)
    pick = (first_ref[...] == column) | (second_ref[...] == column)
    found = exact_dot(pick.astype(jnp.float32), planes)
    lanes = jnp.where(member < PACK, found[:, :LANES], found[:, LANES : 2 * LANES])
    rows = lanes
    for b in range(1, PACK):
        rows = jnp.where(member % PACK == b, turned(lanes, -b), rows)
    lane = lax.broadcasted_iota(jnp.int32, rows.shape, 1)
    count = jnp.where(lane == member * (LANES // GR_DEV), found[:, 2 * LANES :], 0.0)
    count = jnp.sum(count, axis=1, keepdims=True)
    copies = times
    for y in range(out_ref.shape[0] // copies):
        span = slice(y * GR_DEV, (y + 1) * GR_DEV)
        chunk, counts = packed(rows[span], 0), pack_counts(count[span])
        for copy in range(copies):
            store_chunk(out_ref, y * copies + copy, chunk, counts)


def unpack_kernel(in_ref, out_ref):
    slices = out_ref.shape[1] // SLICE
    group = lane_group((GR_DEV, LANES))
    member = lax.broadcasted_iota(jnp.int32, (GR_DEV, LANES), 0) % PACK
    totals = []
    for j in range(slices):
        total = in_ref[j]
        for y in range(1, in_ref.shape[0] // slices):
            total = total + in_ref[y * slices + j]
        totals.append(total)
    count = jnp.where(count_lanes(GR_DEV), jnp.broadcast_to(totals[0][:, 2 * LANES :], (GR_DEV, LANES)), 0.0)
    count = jnp.maximum(jnp.sum(count, axis=1, keepdims=True), 1.0)
    for half in range(slices // PACK):
        result = jnp.zeros((GR_DEV, LANES), jnp.float32)
        for k in range(PACK):
            total = totals[half * PACK + k]
            rows = jnp.concatenate(
                [jnp.broadcast_to(total[:, a * LANES : (a + 1) * LANES], (PACK, LANES)) for a in range(2)], axis=0
            )
            for b in range(PACK):
                result = jnp.where((group == k) & (member == b), turned(rows, k - b), result)
        out_ref[:, half * LANES : (half + 1) * LANES] = result / count


def small_call(kernel, shape, name):
    return pl.pallas_call(
        kernel,
        out_shape=jax.ShapeDtypeStruct(shape, jnp.float32),
        compiler_params=pltpu.CompilerParams(vmem_limit_bytes=16 << 20),
        name=name,
    )


def on_device(visibilities, flags, group_ids, group_order, taper, inv_cov):
    channels = taper.shape[0]
    y_size, z_size, times = (lax.axis_size(axis) for axis in ("y", "z", "ta"))
    block_total = y_size * z_size
    slices = channels // SLICE
    width = GR_DEV * SLICE + LANES

    place = (lax.axis_index(BLOCK_AXES) * 2 + lax.axis_index("ta") % 2)[None]
    blocks = group_sums(visibilities, flags, group_ids, place, block_total)
    blocks = [opposed(block, by) if by else block for block, by in zip(blocks, (-2, -1, 1, 0))]
    parts = transform_parts(taper, inv_cov)

    order = group_order.reshape(y_size, z_size, GR_DEV)
    wanted = lax.dynamic_index_in_dim(order, lax.axis_index("z"), 1, keepdims=False).reshape(-1, 1)
    columns = []
    for core in range(2):
        holder = (wanted // GR_DEV + 2 - core) % block_total
        column = core * z_size + holder % z_size
        columns.append(jnp.where(holder // z_size == lax.axis_index("y"), column, -1))
    parts, *spots = lax.optimization_barrier((parts, *columns, wanted % GR_DEV))

    power = small_call(power_kernel, (z_size * slices, 1, width), "power_rows")(parts, *blocks)
    choose = functools.partial(choose_kernel, times)
    shape = (y_size * times, 1, width)
    chosen = small_call(choose, shape, "choose_rows")(*spots, exchange(power, ("z", "ta")))

    found = exchange(chosen, ("y", "ta"))
    return small_call(unpack_kernel, (GR_DEV, channels), "unpack_rows")(found)


def solution(mesh):
    blocks, times = mesh.devices.shape
    y_size = 2 ** (int(math.log2(blocks)) // 2)
    cut = Mesh(mesh.devices.reshape(y_size, blocks // y_size, times), ("y", "z", "ta"))
    return jax.shard_map(
        on_device,
        mesh=cut,
        in_specs=(P("ta", BLOCK_AXES, None), P("ta", BLOCK_AXES), P(BLOCK_AXES), P(), P(), P()),
        out_specs=P(BLOCK_AXES, None),
        check_vma=False,
    )
```

```python
import functools
import math

import numpy as np
import jax
import jax.numpy as jnp
from jax import lax
from jax.experimental import pallas as pl
from jax.experimental.pallas import tpu as pltpu
from jax.sharding import Mesh
from jax.sharding import PartitionSpec as P

GR_DEV = 8
SPAN = 4
LANES = 128
BLOCK_AXES = ("y", "z")
COUNT_ROWS = 8
SLICE = 32
PACK = 4
TOGETHER = 16


def opposed(shard, by):
    blocks = lax.axis_size(BLOCK_AXES)
    times = lax.axis_size("ta")
    pairs = []
    for block in range(blocks):
        for time in range(times):
            target = (block + (by if time % 2 else -by)) % blocks
            pairs.append((block * times + time, target * times + time))
    return lax.ppermute(shard, (*BLOCK_AXES, "ta"), pairs)


def exchange(chunks, axis):
    return lax.all_to_all(chunks, axis, 0, 0, tiled=True)


def fourier_table(channels):
    ramp = np.arange(channels)
    angles = 2.0 * math.pi / channels * (ramp[:, None] * ramp[None, :] % channels)
    both = np.concatenate([np.cos(angles), np.sin(angles)], axis=1) / math.sqrt(channels)
    return both.astype(np.float32)


def exact_dot(x, y):
    return jnp.dot(x, y, precision=lax.Precision.HIGHEST, preferred_element_type=jnp.float32)


def transform_parts(taper, inv_cov):
    weighted = taper[:, None] * inv_cov
    return exact_dot(weighted, jnp.asarray(fourier_table(taper.shape[0]))).astype(jnp.bfloat16)


BLOCK_STEPS = (3, 2, 0, 1)


def group_kernel(block_total, place_ref, ids_hbm, flags_hbm, vis_hbm, *rest):
    *refs, ids_ref, flags_ref, held_ref, few_sems, sems = rest
    time_count, _, row_width = vis_hbm.shape
    few = [
        pltpu.make_async_copy(source, target, few_sems.at[i])
        for i, (source, target) in enumerate(((ids_hbm, ids_ref), (flags_hbm, flags_ref)))
    ]
    copies = [pltpu.make_async_copy(vis_hbm.at[t], held_ref.at[t], sems.at[t]) for t in range(time_count)]
    for copy in few + copies:
        copy.start()
    for copy in few:
        copy.wait()
    ids = ids_ref[...]
    back = (place_ref[0] >> 1) - (ids >> 3)
    back = jnp.where(back < 0, back + block_total, back)
    back = jnp.where(place_ref[0] & 1 == 0, SPAN - 1 - back, back)
    row = lax.broadcasted_iota(jnp.int32, (SPAN * GR_DEV, ids.shape[1]), 0)
    onehot = (row == back * GR_DEV + (ids & (GR_DEV - 1))).astype(jnp.float32)
    lane = lax.broadcasted_iota(jnp.int32, (SPAN * GR_DEV, LANES), 1)
    counts = jnp.zeros((SPAN * GR_DEV, LANES), jnp.float32)
    for first in range(0, time_count, TOGETHER):
        tables = []
        for t in range(first, first + TOGETHER):
            table = onehot * flags_ref[t : t + 1, :].astype(jnp.float32)
            counts = jnp.where(lane == t, jnp.sum(table, axis=1, keepdims=True), counts)
            tables.append(table.astype(jnp.bfloat16))
        for t in range(first, first + TOGETHER):
            copies[t].wait()
        sums = [
            jnp.dot(table, held_ref[first + i], preferred_element_type=jnp.float32)
            for i, table in enumerate(tables)
        ]
        for step, ref in zip(BLOCK_STEPS, refs):
            span = slice(step * GR_DEV, (step + 1) * GR_DEV)
            both = jnp.concatenate([one[span] for one in sums], axis=0)
            ref[first * GR_DEV : (first + TOGETHER) * GR_DEV, :] = both.astype(jnp.bfloat16)
    for step, ref in zip(BLOCK_STEPS, refs):
        mine = counts[step * GR_DEV : (step + 1) * GR_DEV]
        tile = jnp.concatenate([mine, jnp.zeros((COUNT_ROWS, row_width - LANES), jnp.float32)], axis=1)
        ref[time_count * GR_DEV :, :] = tile.astype(jnp.bfloat16)


def group_sums(visibilities, flags, group_ids, place, block_total):
    time_count, block_length, row_width = visibilities.shape
    block = pltpu.VMEM((time_count * GR_DEV + COUNT_ROWS, row_width), jnp.bfloat16)
    arrays = [pltpu.with_memory_space_constraint(x, pltpu.HBM) for x in (group_ids[None, :], flags, visibilities)]
    return pl.pallas_call(
        functools.partial(group_kernel, block_total),
        in_specs=[pl.BlockSpec(memory_space=pltpu.SMEM)] + [pl.BlockSpec(memory_space=pltpu.HBM)] * len(arrays),
        out_specs=[pl.BlockSpec(memory_space=pltpu.VMEM)] * SPAN,
        out_shape=[block] * SPAN,
        scratch_shapes=[pltpu.VMEM(x.shape, x.dtype) for x in arrays]
        + [pltpu.SemaphoreType.DMA((2,)), pltpu.SemaphoreType.DMA((time_count,))],
        compiler_params=pltpu.CompilerParams(vmem_limit_bytes=16 << 20),
        cost_estimate=pl.CostEstimate(
            flops=2 * time_count * SPAN * GR_DEV * block_length * row_width,
            bytes_accessed=visibilities.size * 2,
            transcendentals=0,
        ),
        name="group_sums",
    )(place, *arrays)


def pair_sum(a, b, c, d):
    return b * a + c * (a + b) + d * (a + b + c)


def lane_group(shape):
    return lax.broadcasted_iota(jnp.int32, shape, len(shape) - 1) // SLICE


def turned(rows, groups):
    return pltpu.roll(rows, groups % PACK * SLICE, 1) if groups % PACK else rows


def packed(rows, slice_index):
    group = lane_group(rows.shape)
    member = lax.broadcasted_iota(jnp.int32, rows.shape, 0) % PACK
    kept = jnp.zeros_like(rows)
    for b in range(PACK):
        kept = jnp.where((group == b) & (member == b), turned(rows, b - slice_index), kept)
    return jnp.concatenate(
        [jnp.sum(kept[a * PACK : (a + 1) * PACK], axis=0, keepdims=True) for a in range(2)], axis=0
    )


def power_kernel(parts_ref, d_ref, c_ref, a_ref, b_ref, out_ref):
    channels = parts_ref.shape[0]
    rows = a_ref.shape[0] - COUNT_ROWS
    slices = channels // SLICE
    cosines = parts_ref[:, :channels]
    sines = parts_ref[:, channels:]

    def dot(x, y):
        return jnp.dot(x, y, preferred_element_type=jnp.float32)

    def delays(ref):
        re, im = ref[:rows, :channels], ref[:rows, channels:]
        return dot(re, cosines) + dot(im, sines), dot(im, cosines) - dot(re, sines)

    blocks = [delays(ref) for ref in (a_ref, b_ref, c_ref, d_ref)]
    pairs = pair_sum(*(re for re, _ in blocks)) + pair_sum(*(im for _, im in blocks))
    power = jnp.sum(pairs.reshape(rows // GR_DEV, GR_DEV, channels), axis=0)
    counts = [ref[rows:, :LANES].astype(jnp.float32) for ref in (a_ref, b_ref, c_ref, d_ref)]
    count = jnp.sum(pair_sum(*counts), axis=1, keepdims=True)
    count = pack_counts(count)
    for j in range(slices):
        half = power[:, j // PACK * LANES : (j // PACK + 1) * LANES]
        chunk = packed(half, j % PACK)
        for copy in range(out_ref.shape[0] // slices):
            store_chunk(out_ref, copy * slices + j, chunk, count)


def count_lanes(rows):
    lane = lax.broadcasted_iota(jnp.int32, (rows, LANES), 1)
    return lane == lax.broadcasted_iota(jnp.int32, (rows, LANES), 0) % GR_DEV * (LANES // GR_DEV)


def pack_counts(count):
    return jnp.sum(jnp.where(count_lanes(GR_DEV), count, 0.0), axis=0, keepdims=True)


def store_chunk(out_ref, index, rows, count):
    out_ref[index, :, :LANES] = rows[:1]
    out_ref[index, :, LANES : 2 * LANES] = rows[1:]
    out_ref[index, :, 2 * LANES :] = count


def choose_kernel(times, first_ref, second_ref, member_ref, in_ref, out_ref):
    planes = []
    for core in range(2):
        for z in range(in_ref.shape[0] // times):
            total = in_ref[z * times + core]
            for time in range(core + 2, times, 2):
                total = total + in_ref[z * times + time]
            planes.append(total)
    planes = jnp.concatenate(planes, axis=0)
    member = member_ref[...]
    column = lax.broadcasted_iota(jnp.int32, (member.shape[0], planes.shape[0]), 1)
    pick = (first_ref[...] == column) | (second_ref[...] == column)
    found = exact_dot(pick.astype(jnp.float32), planes)
    lanes = jnp.where(member < PACK, found[:, :LANES], found[:, LANES : 2 * LANES])
    rows = lanes
    for b in range(1, PACK):
        rows = jnp.where(member % PACK == b, turned(lanes, -b), rows)
    lane = lax.broadcasted_iota(jnp.int32, rows.shape, 1)
    count = jnp.where(lane == member * (LANES // GR_DEV), found[:, 2 * LANES :], 0.0)
    count = jnp.sum(count, axis=1, keepdims=True)
    copies = times
    for y in range(out_ref.shape[0] // copies):
        span = slice(y * GR_DEV, (y + 1) * GR_DEV)
        chunk, counts = packed(rows[span], 0), pack_counts(count[span])
        for copy in range(copies):
            store_chunk(out_ref, y * copies + copy, chunk, counts)


def unpack_kernel(in_ref, out_ref):
    slices = out_ref.shape[1] // SLICE
    group = lane_group((GR_DEV, LANES))
    member = lax.broadcasted_iota(jnp.int32, (GR_DEV, LANES), 0) % PACK
    totals = []
    for j in range(slices):
        total = in_ref[j]
        for y in range(1, in_ref.shape[0] // slices):
            total = total + in_ref[y * slices + j]
        totals.append(total)
    count = jnp.where(count_lanes(GR_DEV), jnp.broadcast_to(totals[0][:, 2 * LANES :], (GR_DEV, LANES)), 0.0)
    count = jnp.maximum(jnp.sum(count, axis=1, keepdims=True), 1.0)
    for half in range(slices // PACK):
        result = jnp.zeros((GR_DEV, LANES), jnp.float32)
        for k in range(PACK):
            total = totals[half * PACK + k]
            rows = jnp.concatenate(
                [jnp.broadcast_to(total[:, a * LANES : (a + 1) * LANES], (PACK, LANES)) for a in range(2)], axis=0
            )
            for b in range(PACK):
                result = jnp.where((group == k) & (member == b), turned(rows, k - b), result)
        out_ref[:, half * LANES : (half + 1) * LANES] = result / count


def small_call(kernel, shape, name):
    return pl.pallas_call(
        kernel,
        out_shape=jax.ShapeDtypeStruct(shape, jnp.float32),
        compiler_params=pltpu.CompilerParams(vmem_limit_bytes=16 << 20),
        name=name,
    )


def on_device(visibilities, flags, group_ids, group_order, taper, inv_cov):
    channels = taper.shape[0]
    y_size, z_size, times = (lax.axis_size(axis) for axis in ("y", "z", "ta"))
    block_total = y_size * z_size
    slices = channels // SLICE
    width = GR_DEV * SLICE + LANES

    place = (lax.axis_index(BLOCK_AXES) * 2 + lax.axis_index("ta") % 2)[None]
    blocks = group_sums(visibilities, flags, group_ids, place, block_total)
    blocks = [opposed(block, by) if by else block for block, by in zip(blocks, (-2, -1, 1, 0))]
    parts = transform_parts(taper, inv_cov)

    order = group_order.reshape(y_size, z_size, GR_DEV)
    wanted = lax.dynamic_index_in_dim(order, lax.axis_index("y"), 0, keepdims=False).reshape(-1, 1)
    columns = []
    for core in range(2):
        holder = (wanted // GR_DEV + 2 - core) % block_total
        column = core * y_size + holder // z_size
        columns.append(jnp.where(holder % z_size == lax.axis_index("z"), column, -1))
    parts, *spots = lax.optimization_barrier((parts, *columns, wanted % GR_DEV))

    power = small_call(power_kernel, (y_size * slices, 1, width), "power_rows")(parts, *blocks)
    choose = functools.partial(choose_kernel, times)
    shape = (z_size * times, 1, width)
    chosen = small_call(choose, shape, "choose_rows")(*spots, exchange(power, ("y", "ta")))

    found = exchange(chosen, ("z", "ta"))
    return small_call(unpack_kernel, (GR_DEV, channels), "unpack_rows")(found)


def solution(mesh):
    blocks, times = mesh.devices.shape
    y_size = 2 ** (int(math.log2(blocks)) // 2)
    cut = Mesh(mesh.devices.reshape(y_size, blocks // y_size, times), ("y", "z", "ta"))
    return jax.shard_map(
        on_device,
        mesh=cut,
        in_specs=(P("ta", BLOCK_AXES, None), P("ta", BLOCK_AXES), P(BLOCK_AXES), P(), P(), P()),
        out_specs=P(BLOCK_AXES, None),
        check_vma=False,
    )
```

```python
import functools
import math

import numpy as np
import jax
import jax.numpy as jnp
from jax import lax
from jax.experimental import pallas as pl
from jax.experimental.pallas import tpu as pltpu
from jax.sharding import Mesh
from jax.sharding import PartitionSpec as P

GR_DEV = 8
SPAN = 4
LANES = 128
BLOCK_AXES = ("y", "z")
COUNT_ROWS = 8
SLICE = 32
PACK = 4
TOGETHER = 16
COPY_TIMES = 2


def opposed(shard, by):
    blocks = lax.axis_size(BLOCK_AXES)
    times = lax.axis_size("ta")
    pairs = []
    for block in range(blocks):
        for time in range(times):
            target = (block + (by if time % 2 else -by)) % blocks
            pairs.append((block * times + time, target * times + time))
    return lax.ppermute(shard, (*BLOCK_AXES, "ta"), pairs)


def exchange(chunks, axis):
    return lax.all_to_all(chunks, axis, 0, 0, tiled=True)


def fourier_table(channels):
    ramp = np.arange(channels)
    angles = 2.0 * math.pi / channels * (ramp[:, None] * ramp[None, :] % channels)
    both = np.concatenate([np.cos(angles), np.sin(angles)], axis=1) / math.sqrt(channels)
    return both.astype(np.float32)


def exact_dot(x, y):
    return jnp.dot(x, y, precision=lax.Precision.HIGHEST, preferred_element_type=jnp.float32)


def transform_parts(taper, inv_cov):
    weighted = taper[:, None] * inv_cov
    return exact_dot(weighted, jnp.asarray(fourier_table(taper.shape[0]))).astype(jnp.bfloat16)


BLOCK_STEPS = (3, 0, 2, 1)


def group_kernel(block_total, place_ref, ids_hbm, flags_hbm, vis_hbm, *rest):
    *refs, ids_ref, flags_ref, held_ref, few_sems, sems = rest
    time_count, _, row_width = vis_hbm.shape
    few = [
        pltpu.make_async_copy(source, target, few_sems.at[i])
        for i, (source, target) in enumerate(((ids_hbm, ids_ref), (flags_hbm, flags_ref)))
    ]
    parts = [pl.ds(t, COPY_TIMES) for t in range(0, time_count, COPY_TIMES)]
    copies = [pltpu.make_async_copy(vis_hbm.at[p], held_ref.at[p], sems.at[i]) for i, p in enumerate(parts)]
    for copy in few + copies:
        copy.start()
    for copy in few:
        copy.wait()
    ids = ids_ref[...]
    back = (place_ref[0] >> 1) - (ids >> 3)
    back = jnp.where(back < 0, back + block_total, back)
    back = jnp.where(place_ref[0] & 1 == 0, SPAN - 1 - back, back)
    row = lax.broadcasted_iota(jnp.int32, (SPAN * GR_DEV, ids.shape[1]), 0)
    onehot = (row == back * GR_DEV + (ids & (GR_DEV - 1))).astype(jnp.float32)
    lane = lax.broadcasted_iota(jnp.int32, (SPAN * GR_DEV, LANES), 1)
    counts = jnp.zeros((SPAN * GR_DEV, LANES), jnp.float32)
    for first in range(0, time_count, TOGETHER):
        tables = []
        for t in range(first, first + TOGETHER):
            table = onehot * flags_ref[t : t + 1, :].astype(jnp.float32)
            counts = jnp.where(lane == t, jnp.sum(table, axis=1, keepdims=True), counts)
            tables.append(table.astype(jnp.bfloat16))
        for copy in copies[first // COPY_TIMES : (first + TOGETHER) // COPY_TIMES]:
            copy.wait()
        sums = [
            jnp.dot(table, held_ref[first + i], preferred_element_type=jnp.float32)
            for i, table in enumerate(tables)
        ]
        for step, ref in zip(BLOCK_STEPS, refs):
            span = slice(step * GR_DEV, (step + 1) * GR_DEV)
            both = jnp.concatenate([one[span] for one in sums], axis=0)
            ref[first * GR_DEV : (first + TOGETHER) * GR_DEV, :] = both.astype(jnp.bfloat16)
    for step, ref in zip(BLOCK_STEPS, refs):
        mine = counts[step * GR_DEV : (step + 1) * GR_DEV]
        tile = jnp.concatenate([mine, jnp.zeros((COUNT_ROWS, row_width - LANES), jnp.float32)], axis=1)
        ref[time_count * GR_DEV :, :] = tile.astype(jnp.bfloat16)


def group_sums(visibilities, flags, group_ids, place, block_total):
    time_count, block_length, row_width = visibilities.shape
    block = pltpu.VMEM((time_count * GR_DEV + COUNT_ROWS, row_width), jnp.bfloat16)
    arrays = [pltpu.with_memory_space_constraint(x, pltpu.HBM) for x in (group_ids[None, :], flags, visibilities)]
    return pl.pallas_call(
        functools.partial(group_kernel, block_total),
        in_specs=[pl.BlockSpec(memory_space=pltpu.SMEM)] + [pl.BlockSpec(memory_space=pltpu.HBM)] * len(arrays),
        out_specs=[pl.BlockSpec(memory_space=pltpu.VMEM)] * SPAN,
        out_shape=[block] * SPAN,
        scratch_shapes=[pltpu.VMEM(x.shape, x.dtype) for x in arrays]
        + [pltpu.SemaphoreType.DMA((2,)), pltpu.SemaphoreType.DMA((time_count // COPY_TIMES,))],
        compiler_params=pltpu.CompilerParams(vmem_limit_bytes=16 << 20),
        cost_estimate=pl.CostEstimate(
            flops=2 * time_count * SPAN * GR_DEV * block_length * row_width,
            bytes_accessed=visibilities.size * 2,
            transcendentals=0,
        ),
        name="group_sums",
    )(place, *arrays)


def pair_sum(a, b, c, d):
    return b * a + c * (a + b) + d * (a + b + c)


def lane_group(shape):
    return lax.broadcasted_iota(jnp.int32, shape, len(shape) - 1) // SLICE


def turned(rows, groups):
    return pltpu.roll(rows, groups % PACK * SLICE, 1) if groups % PACK else rows


def packed(rows, slice_index):
    group = lane_group(rows.shape)
    member = lax.broadcasted_iota(jnp.int32, rows.shape, 0) % PACK
    kept = jnp.zeros_like(rows)
    for b in range(PACK):
        kept = jnp.where((group == b) & (member == b), turned(rows, b - slice_index), kept)
    return jnp.concatenate(
        [jnp.sum(kept[a * PACK : (a + 1) * PACK], axis=0, keepdims=True) for a in range(2)], axis=0
    )


def power_kernel(parts_ref, d_ref, a_ref, c_ref, b_ref, out_ref):
    channels = parts_ref.shape[0]
    rows = a_ref.shape[0] - COUNT_ROWS
    slices = channels // SLICE
    cosines = parts_ref[:, :channels]
    sines = parts_ref[:, channels:]

    def dot(x, y):
        return jnp.dot(x, y, preferred_element_type=jnp.float32)

    def delays(ref):
        re, im = ref[:rows, :channels], ref[:rows, channels:]
        return dot(re, cosines) + dot(im, sines), dot(im, cosines) - dot(re, sines)

    blocks = [delays(ref) for ref in (a_ref, b_ref, c_ref, d_ref)]
    pairs = pair_sum(*(re for re, _ in blocks)) + pair_sum(*(im for _, im in blocks))
    power = jnp.sum(pairs.reshape(rows // GR_DEV, GR_DEV, channels), axis=0)
    counts = [ref[rows:, :LANES].astype(jnp.float32) for ref in (a_ref, b_ref, c_ref, d_ref)]
    count = jnp.sum(pair_sum(*counts), axis=1, keepdims=True)
    count = pack_counts(count)
    for j in range(slices):
        half = power[:, j // PACK * LANES : (j // PACK + 1) * LANES]
        chunk = packed(half, j % PACK)
        for copy in range(out_ref.shape[0] // slices):
            store_chunk(out_ref, copy * slices + j, chunk, count)


def count_lanes(rows):
    lane = lax.broadcasted_iota(jnp.int32, (rows, LANES), 1)
    return lane == lax.broadcasted_iota(jnp.int32, (rows, LANES), 0) % GR_DEV * (LANES // GR_DEV)


def pack_counts(count):
    return jnp.sum(jnp.where(count_lanes(GR_DEV), count, 0.0), axis=0, keepdims=True)


def store_chunk(out_ref, index, rows, count):
    out_ref[index, :, :LANES] = rows[:1]
    out_ref[index, :, LANES : 2 * LANES] = rows[1:]
    out_ref[index, :, 2 * LANES :] = count


def choose_kernel(times, first_ref, second_ref, member_ref, in_ref, out_ref):
    planes = []
    for core in range(2):
        for z in range(in_ref.shape[0] // times):
            total = in_ref[z * times + core]
            for time in range(core + 2, times, 2):
                total = total + in_ref[z * times + time]
            planes.append(total)
    planes = jnp.concatenate(planes, axis=0)
    member = member_ref[...]
    column = lax.broadcasted_iota(jnp.int32, (member.shape[0], planes.shape[0]), 1)
    pick = (first_ref[...] == column) | (second_ref[...] == column)
    found = exact_dot(pick.astype(jnp.float32), planes)
    lanes = jnp.where(member < PACK, found[:, :LANES], found[:, LANES : 2 * LANES])
    rows = lanes
    for b in range(1, PACK):
        rows = jnp.where(member % PACK == b, turned(lanes, -b), rows)
    lane = lax.broadcasted_iota(jnp.int32, rows.shape, 1)
    count = jnp.where(lane == member * (LANES // GR_DEV), found[:, 2 * LANES :], 0.0)
    count = jnp.sum(count, axis=1, keepdims=True)
    copies = times
    for y in range(out_ref.shape[0] // copies):
        span = slice(y * GR_DEV, (y + 1) * GR_DEV)
        chunk, counts = packed(rows[span], 0), pack_counts(count[span])
        for copy in range(copies):
            store_chunk(out_ref, y * copies + copy, chunk, counts)


def unpack_kernel(in_ref, out_ref):
    slices = out_ref.shape[1] // SLICE
    group = lane_group((GR_DEV, LANES))
    member = lax.broadcasted_iota(jnp.int32, (GR_DEV, LANES), 0) % PACK
    totals = []
    for j in range(slices):
        total = in_ref[j]
        for y in range(1, in_ref.shape[0] // slices):
            total = total + in_ref[y * slices + j]
        totals.append(total)
    count = jnp.where(count_lanes(GR_DEV), jnp.broadcast_to(totals[0][:, 2 * LANES :], (GR_DEV, LANES)), 0.0)
    count = jnp.maximum(jnp.sum(count, axis=1, keepdims=True), 1.0)
    for half in range(slices // PACK):
        result = jnp.zeros((GR_DEV, LANES), jnp.float32)
        for k in range(PACK):
            total = totals[half * PACK + k]
            rows = jnp.concatenate(
                [jnp.broadcast_to(total[:, a * LANES : (a + 1) * LANES], (PACK, LANES)) for a in range(2)], axis=0
            )
            for b in range(PACK):
                result = jnp.where((group == k) & (member == b), turned(rows, k - b), result)
        out_ref[:, half * LANES : (half + 1) * LANES] = result / count


def small_call(kernel, shape, name):
    return pl.pallas_call(
        kernel,
        out_shape=jax.ShapeDtypeStruct(shape, jnp.float32),
        compiler_params=pltpu.CompilerParams(vmem_limit_bytes=16 << 20),
        name=name,
    )


def on_device(visibilities, flags, group_ids, group_order, taper, inv_cov):
    channels = taper.shape[0]
    y_size, z_size, times = (lax.axis_size(axis) for axis in ("y", "z", "ta"))
    block_total = y_size * z_size
    slices = channels // SLICE
    width = GR_DEV * SLICE + LANES

    place = (lax.axis_index(BLOCK_AXES) * 2 + lax.axis_index("ta") % 2)[None]
    blocks = group_sums(visibilities, flags, group_ids, place, block_total)
    blocks = [opposed(block, by) if by else block for block, by in zip(blocks, (-2, 1, -1, 0))]
    parts = transform_parts(taper, inv_cov)

    order = group_order.reshape(y_size, z_size, GR_DEV)
    wanted = lax.dynamic_index_in_dim(order, lax.axis_index("z"), 1, keepdims=False).reshape(-1, 1)
    columns = []
    for core in range(2):
        holder = (wanted // GR_DEV + 2 - core) % block_total
        column = core * z_size + holder % z_size
        columns.append(jnp.where(holder // z_size == lax.axis_index("y"), column, -1))
    parts, *spots = lax.optimization_barrier((parts, *columns, wanted % GR_DEV))

    power = small_call(power_kernel, (z_size * slices, 1, width), "power_rows")(parts, *blocks)
    choose = functools.partial(choose_kernel, times)
    shape = (y_size * times, 1, width)
    chosen = small_call(choose, shape, "choose_rows")(*spots, exchange(power, ("z", "ta")))

    found = exchange(chosen, ("y", "ta"))
    return small_call(unpack_kernel, (GR_DEV, channels), "unpack_rows")(found)


def solution(mesh):
    blocks, times = mesh.devices.shape
    y_size = 2 ** (int(math.log2(blocks)) // 2)
    cut = Mesh(mesh.devices.reshape(y_size, blocks // y_size, times), ("y", "z", "ta"))
    return jax.shard_map(
        on_device,
        mesh=cut,
        in_specs=(P("ta", BLOCK_AXES, None), P("ta", BLOCK_AXES), P(BLOCK_AXES), P(), P(), P()),
        out_specs=P(BLOCK_AXES, None),
        check_vma=False,
    )
```

```python
import functools
import math

import numpy as np
import jax
import jax.numpy as jnp
from jax import lax
from jax.experimental import pallas as pl
from jax.experimental.pallas import tpu as pltpu
from jax.sharding import Mesh
from jax.sharding import PartitionSpec as P

GR_DEV = 8
SPAN = 4
LANES = 128
BLOCK_AXES = ("y", "z")
TIME_AXES = ("x", "core")
COUNT_ROWS = 8
SLICE = 32
PACK = 4
TOGETHER = 16


def opposed(shard, by):
    blocks = lax.axis_size(BLOCK_AXES)
    times = lax.axis_size(TIME_AXES)
    pairs = []
    for block in range(blocks):
        for time in range(times):
            target = (block + (by if time % 2 else -by)) % blocks
            pairs.append((block * times + time, target * times + time))
    return lax.ppermute(shard, (*BLOCK_AXES, *TIME_AXES), pairs)


def exchange(chunks, axis):
    return lax.all_to_all(chunks, axis, 0, 0, tiled=True)


def fourier_table(channels):
    ramp = np.arange(channels)
    angles = 2.0 * math.pi / channels * (ramp[:, None] * ramp[None, :] % channels)
    both = np.concatenate([np.cos(angles), np.sin(angles)], axis=1) / math.sqrt(channels)
    return both.astype(np.float32)


def exact_dot(x, y):
    return jnp.dot(x, y, precision=lax.Precision.HIGHEST, preferred_element_type=jnp.float32)


def transform_parts(taper, inv_cov):
    weighted = taper[:, None] * inv_cov
    return exact_dot(weighted, jnp.asarray(fourier_table(taper.shape[0]))).astype(jnp.bfloat16)


BLOCK_STEPS = (3, 2, 0, 1)


def group_kernel(block_total, place_ref, ids_hbm, flags_hbm, vis_hbm, *rest):
    *refs, ids_ref, flags_ref, held_ref, few_sems, sems = rest
    time_count, _, row_width = vis_hbm.shape
    few = [
        pltpu.make_async_copy(source, target, few_sems.at[i])
        for i, (source, target) in enumerate(((ids_hbm, ids_ref), (flags_hbm, flags_ref)))
    ]
    copies = [pltpu.make_async_copy(vis_hbm.at[t], held_ref.at[t], sems.at[t]) for t in range(time_count)]
    for copy in few + copies:
        copy.start()
    for copy in few:
        copy.wait()
    ids = ids_ref[...]
    back = (place_ref[0] >> 1) - (ids >> 3)
    back = jnp.where(back < 0, back + block_total, back)
    back = jnp.where(place_ref[0] & 1 == 0, SPAN - 1 - back, back)
    row = lax.broadcasted_iota(jnp.int32, (SPAN * GR_DEV, ids.shape[1]), 0)
    onehot = (row == back * GR_DEV + (ids & (GR_DEV - 1))).astype(jnp.float32)
    lane = lax.broadcasted_iota(jnp.int32, (SPAN * GR_DEV, LANES), 1)
    counts = jnp.zeros((SPAN * GR_DEV, LANES), jnp.float32)
    for first in range(0, time_count, TOGETHER):
        tables = []
        for t in range(first, first + TOGETHER):
            table = onehot * flags_ref[t : t + 1, :].astype(jnp.float32)
            counts = jnp.where(lane == t, jnp.sum(table, axis=1, keepdims=True), counts)
            tables.append(table.astype(jnp.bfloat16))
        for t in range(first, first + TOGETHER):
            copies[t].wait()
        sums = [
            jnp.dot(table, held_ref[first + i], preferred_element_type=jnp.float32)
            for i, table in enumerate(tables)
        ]
        for step, ref in zip(BLOCK_STEPS, refs):
            span = slice(step * GR_DEV, (step + 1) * GR_DEV)
            both = jnp.concatenate([one[span] for one in sums], axis=0)
            ref[first * GR_DEV : (first + TOGETHER) * GR_DEV, :] = both.astype(jnp.bfloat16)
    for step, ref in zip(BLOCK_STEPS, refs):
        mine = counts[step * GR_DEV : (step + 1) * GR_DEV]
        tile = jnp.concatenate([mine, jnp.zeros((COUNT_ROWS, row_width - LANES), jnp.float32)], axis=1)
        ref[time_count * GR_DEV :, :] = tile.astype(jnp.bfloat16)


def group_sums(visibilities, flags, group_ids, place, block_total):
    time_count, block_length, row_width = visibilities.shape
    block = pltpu.VMEM((time_count * GR_DEV + COUNT_ROWS, row_width), jnp.bfloat16)
    arrays = [pltpu.with_memory_space_constraint(x, pltpu.HBM) for x in (group_ids[None, :], flags, visibilities)]
    return pl.pallas_call(
        functools.partial(group_kernel, block_total),
        in_specs=[pl.BlockSpec(memory_space=pltpu.SMEM)] + [pl.BlockSpec(memory_space=pltpu.HBM)] * len(arrays),
        out_specs=[pl.BlockSpec(memory_space=pltpu.VMEM)] * SPAN,
        out_shape=[block] * SPAN,
        scratch_shapes=[pltpu.VMEM(x.shape, x.dtype) for x in arrays]
        + [pltpu.SemaphoreType.DMA((2,)), pltpu.SemaphoreType.DMA((time_count,))],
        compiler_params=pltpu.CompilerParams(vmem_limit_bytes=16 << 20),
        cost_estimate=pl.CostEstimate(
            flops=2 * time_count * SPAN * GR_DEV * block_length * row_width,
            bytes_accessed=visibilities.size * 2,
            transcendentals=0,
        ),
        name="group_sums",
    )(place, *arrays)


def pair_sum(a, b, c, d):
    return b * a + c * (a + b) + d * (a + b + c)


def lane_group(shape):
    return lax.broadcasted_iota(jnp.int32, shape, len(shape) - 1) // SLICE


def turned(rows, groups):
    return pltpu.roll(rows, groups % PACK * SLICE, 1) if groups % PACK else rows


def packed(rows, slice_index):
    group = lane_group(rows.shape)
    member = lax.broadcasted_iota(jnp.int32, rows.shape, 0) % PACK
    kept = jnp.zeros_like(rows)
    for b in range(PACK):
        kept = jnp.where((group == b) & (member == b), turned(rows, b - slice_index), kept)
    return jnp.concatenate(
        [jnp.sum(kept[a * PACK : (a + 1) * PACK], axis=0, keepdims=True) for a in range(2)], axis=0
    )


def power_kernel(parts_ref, d_ref, c_ref, a_ref, b_ref, out_ref):
    channels = parts_ref.shape[0]
    rows = a_ref.shape[0] - COUNT_ROWS
    slices = channels // SLICE
    cosines = parts_ref[:, :channels]
    sines = parts_ref[:, channels:]

    def dot(x, y):
        return jnp.dot(x, y, preferred_element_type=jnp.float32)

    def delays(ref):
        re, im = ref[:rows, :channels], ref[:rows, channels:]
        return dot(re, cosines) + dot(im, sines), dot(im, cosines) - dot(re, sines)

    blocks = [delays(ref) for ref in (a_ref, b_ref, c_ref, d_ref)]
    pairs = pair_sum(*(re for re, _ in blocks)) + pair_sum(*(im for _, im in blocks))
    power = jnp.sum(pairs.reshape(rows // GR_DEV, GR_DEV, channels), axis=0)
    counts = [ref[rows:, :LANES].astype(jnp.float32) for ref in (a_ref, b_ref, c_ref, d_ref)]
    count = jnp.sum(pair_sum(*counts), axis=1, keepdims=True)
    count = pack_counts(count)
    for j in range(slices):
        half = power[:, j % 2 * LANES : (j % 2 + 1) * LANES]
        chunk = packed(half, j // 2)
        for copy in range(out_ref.shape[0] // slices):
            store_chunk(out_ref, copy * slices + j, chunk, count)


def count_lanes(rows):
    lane = lax.broadcasted_iota(jnp.int32, (rows, LANES), 1)
    return lane == lax.broadcasted_iota(jnp.int32, (rows, LANES), 0) % GR_DEV * (LANES // GR_DEV)


def pack_counts(count):
    return jnp.sum(jnp.where(count_lanes(GR_DEV), count, 0.0), axis=0, keepdims=True)


def store_chunk(out_ref, index, rows, count):
    out_ref[index, :, :LANES] = rows[:1]
    out_ref[index, :, LANES : 2 * LANES] = rows[1:]
    out_ref[index, :, 2 * LANES :] = count


def choose_kernel(times, first_ref, second_ref, member_ref, in_ref, out_ref):
    planes = []
    for core in range(2):
        for z in range(in_ref.shape[0] // times):
            total = in_ref[z * times + core]
            for time in range(core + 2, times, 2):
                total = total + in_ref[z * times + time]
            planes.append(total)
    planes = jnp.concatenate(planes, axis=0)
    member = member_ref[...]
    column = lax.broadcasted_iota(jnp.int32, (member.shape[0], planes.shape[0]), 1)
    pick = (first_ref[...] == column) | (second_ref[...] == column)
    found = exact_dot(pick.astype(jnp.float32), planes)
    lanes = jnp.where(member < PACK, found[:, :LANES], found[:, LANES : 2 * LANES])
    rows = lanes
    for b in range(1, PACK):
        rows = jnp.where(member % PACK == b, turned(lanes, -b), rows)
    lane = lax.broadcasted_iota(jnp.int32, rows.shape, 1)
    count = jnp.where(lane == member * (LANES // GR_DEV), found[:, 2 * LANES :], 0.0)
    count = jnp.sum(count, axis=1, keepdims=True)
    copies = times // 2
    for y in range(out_ref.shape[0] // copies):
        span = slice(y * GR_DEV, (y + 1) * GR_DEV)
        chunk, counts = packed(rows[span], 0), pack_counts(count[span])
        for copy in range(copies):
            store_chunk(out_ref, y * copies + copy, chunk, counts)


def unpack_kernel(in_ref, out_ref):
    group = lane_group((GR_DEV, LANES))
    member = lax.broadcasted_iota(jnp.int32, (GR_DEV, LANES), 0) % PACK
    result = jnp.zeros((GR_DEV, LANES), jnp.float32)
    for k in range(PACK):
        total = in_ref[k]
        for y in range(1, in_ref.shape[0] // PACK):
            total = total + in_ref[y * PACK + k]
        rows = jnp.concatenate(
            [jnp.broadcast_to(total[:, a * LANES : (a + 1) * LANES], (PACK, LANES)) for a in range(2)], axis=0
        )
        for b in range(PACK):
            result = jnp.where((group == k) & (member == b), turned(rows, k - b), result)
    count = jnp.where(count_lanes(GR_DEV), jnp.broadcast_to(total[:, 2 * LANES :], (GR_DEV, LANES)), 0.0)
    out_ref[...] = result / jnp.maximum(jnp.sum(count, axis=1, keepdims=True), 1.0)


def small_call(kernel, shape, name):
    return pl.pallas_call(
        kernel,
        out_shape=jax.ShapeDtypeStruct(shape, jnp.float32),
        compiler_params=pltpu.CompilerParams(vmem_limit_bytes=16 << 20),
        name=name,
    )


def on_device(visibilities, flags, group_ids, group_order, taper, inv_cov):
    channels = taper.shape[0]
    y_size, z_size, times = (lax.axis_size(axis) for axis in ("y", "z", TIME_AXES))
    block_total = y_size * z_size
    slices = channels // SLICE
    width = GR_DEV * SLICE + LANES

    core = lax.axis_index("core")
    place = (lax.axis_index(BLOCK_AXES) * 2 + core)[None]
    blocks = group_sums(visibilities, flags, group_ids, place, block_total)
    blocks = [opposed(block, by) if by else block for block, by in zip(blocks, (-2, -1, 1, 0))]
    parts = transform_parts(taper, inv_cov)

    order = group_order.reshape(y_size, z_size, GR_DEV)
    wanted = lax.dynamic_index_in_dim(order, lax.axis_index("z"), 1, keepdims=False).reshape(-1, 1)
    columns = []
    for side in range(2):
        holder = (wanted // GR_DEV + 2 - side) % block_total
        column = side * z_size + holder % z_size
        columns.append(jnp.where(holder // z_size == lax.axis_index("y"), column, -1))
    parts, *spots = lax.optimization_barrier((parts, *columns, wanted % GR_DEV))

    power = small_call(power_kernel, (z_size * slices, 1, width), "power_rows")(parts, *blocks)
    choose = functools.partial(choose_kernel, times)
    shape = (y_size * times // 2, 1, width)
    chosen = small_call(choose, shape, "choose_rows")(*spots, exchange(power, ("z", *TIME_AXES)))

    found = exchange(chosen, ("y", "x"))
    mine = small_call(unpack_kernel, (GR_DEV, LANES), "unpack_rows")(found)
    other = lax.ppermute(mine, "core", [(0, 1), (1, 0)])
    first = core == 0
    return jnp.concatenate([jnp.where(first, mine, other), jnp.where(first, other, mine)], axis=1)


def solution(mesh):
    blocks, times = mesh.devices.shape
    y_size = 2 ** (int(math.log2(blocks)) // 2)
    cut = Mesh(
        mesh.devices.reshape(y_size, blocks // y_size, times // 2, 2), (*BLOCK_AXES, *TIME_AXES)
    )
    return jax.shard_map(
        on_device,
        mesh=cut,
        in_specs=(P(TIME_AXES, BLOCK_AXES, None), P(TIME_AXES, BLOCK_AXES), P(BLOCK_AXES), P(), P(), P()),
        out_specs=P(BLOCK_AXES, None),
        check_vma=False,
    )
```
